256 devices in a mesh: dp: 8 (over y_hi, x), tensor: 32 (over z, y_lo, core).
Axes of the slice: x: 4, y: 4 (y_hi: 2, y_lo: 2; y = y_hi * 2 + y_lo), z: 8, core: 2. Of those that a mesh axis runs over, the one named last changes fastest.
Arguments:
- tokens: bfloat16 [1024, 8192], P(('dp', 'tensor')), may hold values from -6 to 6
- grad_out: bfloat16 [1024, 8192], P(('dp', 'tensor')), may hold values from -6 to 6
- w1_blocks: bfloat16 [2048, 128, 128], P('tensor'), may hold values from -0.125 to 0.125
- w1_rows: int32 [2048], P('tensor'), may hold values from 0 to 63, as said below
- w1_cols: int32 [2048], P('tensor'), may hold values from 0 to 127, as said below
- w1_count: int32 [32], P('tensor'), may hold values from 21 to 64, as said below
- w2_blocks: bfloat16 [2048, 128, 128], P('tensor'), may hold values from -0.09375 to 0.09375
- w2_rows: int32 [2048], P('tensor'), may hold values from 0 to 127, as said below
- w2_cols: int32 [2048], P('tensor'), may hold values from 0 to 63
- w2_count: int32 [32], P('tensor'), may hold values from 21 to 64, as said below
Outputs:
- layer_out: bfloat16 [1024, 8192], P(('dp', 'tensor'))
- grad_tokens: bfloat16 [1024, 8192], P(('dp', 'tensor'))
- grad_w1: float32 [2048, 128, 128], P('tensor', 'dp')
- grad_w2: float32 [2048, 128, 128], P('tensor', 'dp')
The draws below stay inside these ranges and needn't reach their ends.
Inputs may be any that keep to these rules, and one draw needn't show every extreme that they name: `w1_rows`: the slots of stripe t hold distinct (row, column) block pairs; for the up projection the block columns lie in t * 4 to t * 4 + 3. `w1_cols`: block columns of stripe t lie in t * 4 to t * 4 + 3. `w1_count`: some stripe has all 64 slots live. `w2_rows`: block rows of stripe t lie in t * 4 to t * 4 + 3; the slots of a stripe hold distinct (row, column) block pairs. `w2_count`: some stripe has all 64 slots live.
All inputs are finite; a program needn't handle non-finite values.
Results may differ from the reference program's by a relative error of at most 0.023.
Values may be sent and summed in bfloat16 or wider, within the bound.
No kernel may reach another device: no remote copies, remote signals or barrier semaphores. Data moves between devices by JAX's collectives and lax.ppermute only.
A program may use at most 128 MiB of HBM per device.

```python
import jax
import jax.numpy as jnp
from jax import lax

D = 8192
FF = 16384
BLK = 128
TOK_DEV = 128
TOKENS = 1024
DB = 64
SB = 4
CAP = 64
N_DP = 8
N_TENSOR = 32


def block_places(key, salt):
    key = jax.random.fold_in(key, salt)
    stripe_keys = jax.random.split(key, N_TENSOR)
    places = jax.vmap(lambda one_key: jax.random.permutation(one_key, DB * SB))(stripe_keys)[:, :CAP]
    stripe = jnp.arange(N_TENSOR, dtype=jnp.int32)[:, None]
    return (places.astype(jnp.int32), stripe)


def live_counts(key, salt):
    key = jax.random.fold_in(key, salt)
    first_key, second_key = jax.random.split(key)
    counts = jax.random.randint(first_key, (N_TENSOR,), CAP // 3, CAP + 1, dtype=jnp.int32)
    fullest = jax.random.randint(second_key, (), 0, N_TENSOR, dtype=jnp.int32)
    return counts.at[fullest].set(CAP)


def draw_w1_rows(key, part):
    places, stripe = block_places(key, 11)
    return (places // SB).reshape(N_TENSOR * CAP)


def draw_w1_cols(key, part):
    places, stripe = block_places(key, 11)
    return (stripe * SB + places % SB).reshape(N_TENSOR * CAP)


def draw_w2_rows(key, part):
    places, stripe = block_places(key, 12)
    return (stripe * SB + places // DB).reshape(N_TENSOR * CAP)


def draw_w2_cols(key, part):
    places, stripe = block_places(key, 12)
    return (places % DB).reshape(N_TENSOR * CAP)


def draw_w1_count(key, part):
    return live_counts(key, 21)


def draw_w2_count(key, part):
    return live_counts(key, 22)


def levels(key, shape, pieces, smallest, high):
    factor_of = 1.0
    for dim, blocks in pieces:
        draws = jax.random.uniform(jax.random.fold_in(jax.random.fold_in(key, 6), dim), (blocks,), jnp.float32, smallest / len(pieces), high / len(pieces))
        factor_of = factor_of * jnp.repeat(jnp.exp(draws), shape[dim] // blocks).reshape((-1,) + (1,) * (len(shape) - 1 - dim))
    return factor_of


def normal_values(rng, dims, width, bound, cuts=(), kind=jnp.bfloat16):
    drawn = width * jax.random.normal(rng, dims, jnp.float32)
    if cuts:
        drawn = drawn * levels(rng, dims, cuts, -0.22, 0.18)
    return jnp.clip(drawn, -bound, bound).astype(kind)


def setup_inputs(seed: int = 0) -> dict:
    seeds = jax.random.split(jax.random.key(seed), 11)
    return {
        "tokens": normal_values(seeds[0], (TOKENS, D), 1.0, 6.0, ((0, 256),)),
        "grad_out": normal_values(seeds[1], (TOKENS, D), 1.0, 6.0, ((0, 256),)),
        "w1_blocks": normal_values(seeds[2], (N_TENSOR * CAP, BLK, BLK), (D // 4) ** -0.5, 0.125, ((0, 32),)),
        "w1_rows": draw_w1_rows(jax.random.fold_in(seeds[10], 71), 0),
        "w1_cols": draw_w1_cols(jax.random.fold_in(seeds[10], 71), 0),
        "w1_count": draw_w1_count(jax.random.fold_in(seeds[10], 71), 0),
        "w2_blocks": normal_values(seeds[6], (N_TENSOR * CAP, BLK, BLK), (FF // 4) ** -0.5, 0.09375, ((0, 32),)),
        "w2_rows": draw_w2_rows(jax.random.fold_in(seeds[10], 71), 0),
        "w2_cols": draw_w2_cols(jax.random.fold_in(seeds[10], 71), 0),
        "w2_count": draw_w2_count(jax.random.fold_in(seeds[10], 71), 0),
    }


HIGHEST = lax.Precision.HIGHEST

def gelu_tanh(values):
    return jax.nn.gelu(values, approximate=True)

def selector(labels, label_width):
    return (labels[:, None] == jnp.arange(label_width, dtype=jnp.int32)[None, :]).astype(jnp.float32)

def rounded(values):
    narrow = lax.optimization_barrier(values.astype(jnp.bfloat16))
    return narrow.astype(jnp.float32)

def reference(tokens, grad_out, w1_blocks, w1_rows, w1_cols, w1_count, w2_blocks, w2_rows, w2_cols, w2_count):
    slot_ids = jnp.arange(CAP, dtype=jnp.int32)
    token_grid = tokens.reshape(TOKENS, DB, BLK)
    grad_grid = grad_out.reshape(TOKENS, DB, BLK)
    stacked = (w1_blocks.reshape(N_TENSOR, CAP, BLK, BLK), w1_rows.reshape(N_TENSOR, CAP), w1_cols.reshape(N_TENSOR, CAP), w1_count, w2_blocks.reshape(N_TENSOR, CAP, BLK, BLK), w2_rows.reshape(N_TENSOR, CAP), w2_cols.reshape(N_TENSOR, CAP), w2_count, jnp.arange(N_TENSOR, dtype=jnp.int32))

    def one_stripe(carry, inputs):
        out_sum, back_sum = carry
        first_raw, first_rowids, first_colids, first_live, second_raw, second_rowids, second_colids, second_live, stripe = inputs
        live_first = (slot_ids < first_live).astype(jnp.float32)
        live_second = (slot_ids < second_live).astype(jnp.float32)
        first_kept = (first_raw * live_first.astype(jnp.bfloat16)[:, None, None]).astype(jnp.float32)
        second_kept = (second_raw * live_second.astype(jnp.bfloat16)[:, None, None]).astype(jnp.float32)
        first_colsel = selector(first_colids - stripe * SB, SB)
        first_rowsel = selector(first_rowids, DB)
        second_rowsel = selector(second_rowids - stripe * SB, SB)
        second_colsel = selector(second_colids, DB)
        token_blocks = jnp.take(token_grid, first_rowids, axis=1)
        products = jnp.einsum('tsk,skj->tsj', token_blocks.astype(jnp.float32), first_kept)
        preact = jnp.einsum('tsj,sc->tcj', products, first_colsel, precision=HIGHEST)
        hidden = gelu_tanh(preact).astype(jnp.bfloat16)
        hidden_blocks = jnp.einsum('tcj,sc->tsj', hidden.astype(jnp.float32), second_rowsel, precision=HIGHEST).astype(jnp.bfloat16)
        out_products = jnp.einsum('tsk,skj->tsj', hidden_blocks.astype(jnp.float32), second_kept)
        out_part = jnp.einsum('tsj,sd->tdj', out_products, second_colsel, precision=HIGHEST).reshape(TOKENS, D)
        grad_blocks = jnp.take(grad_grid, second_colids, axis=1)
        back_hidden = jnp.einsum('tsj,skj->tsk', grad_blocks.astype(jnp.float32), second_kept)
        grad_hidden = jnp.einsum('tsk,sr->trk', back_hidden, second_rowsel, precision=HIGHEST)
        unused, pullback = jax.vjp(gelu_tanh, preact)
        grad_pre = pullback(grad_hidden)[0].astype(jnp.bfloat16)
        grad_pre_blocks = jnp.einsum('tcj,sc->tsj', grad_pre.astype(jnp.float32), first_colsel, precision=HIGHEST).astype(jnp.bfloat16)
        back_products = jnp.einsum('tsj,skj->tsk', grad_pre_blocks.astype(jnp.float32), first_kept)
        back_part = jnp.einsum('tsk,sr->trk', back_products, first_rowsel, precision=HIGHEST).reshape(TOKENS, D)
        shard_first = jnp.einsum('gtsk,gtsj->gskj', token_blocks.reshape(N_DP, TOK_DEV, CAP, BLK).astype(jnp.float32), grad_pre_blocks.reshape(N_DP, TOK_DEV, CAP, BLK).astype(jnp.float32))
        shard_second = jnp.einsum('gtsk,gtsj->gskj', hidden_blocks.reshape(N_DP, TOK_DEV, CAP, BLK).astype(jnp.float32), grad_blocks.reshape(N_DP, TOK_DEV, CAP, BLK).astype(jnp.float32))
        first_grad = lax.optimization_barrier(jnp.sum(rounded(shard_first), axis=0)) * live_first[:, None, None]
        second_grad = lax.optimization_barrier(jnp.sum(rounded(shard_second), axis=0)) * live_second[:, None, None]
        return ((out_sum + rounded(out_part), back_sum + rounded(back_part)), (first_grad, second_grad))
    zeros_start = jnp.zeros((TOKENS, D), jnp.float32)
    sums, grads = lax.scan(one_stripe, (zeros_start, zeros_start), stacked)
    layer_out = sums[0].astype(jnp.bfloat16)
    grad_tokens = sums[1].astype(jnp.bfloat16)
    grad_w1 = grads[0].reshape(N_TENSOR * CAP, BLK, BLK)
    grad_w2 = grads[1].reshape(N_TENSOR * CAP, BLK, BLK)
    return (layer_out, grad_tokens, grad_w1, grad_w2)
```

```python
import functools

import jax
import jax.numpy as jnp
from jax import lax
from jax.experimental import pallas as pl
from jax.experimental.pallas import tpu as pltpu
from jax.sharding import Mesh
from jax.sharding import PartitionSpec as P

AXES = ("yh", "x", "z", "yl", "c")
SIZES = (2, 4, 8, 2, 2)
BLK = 128
SB = 4
CAP = 64
HALF = 32
F32 = jnp.float32
BF16 = jnp.bfloat16
GROUP = 8
R1, C1, R2, C2, LIVE1, LIVE2, CORE, PX, PYH = 0, 64, 128, 192, 256, 257, 258, 259, 260


def gelu_pair(v):
    a = 0.7978845608028654
    b = 0.044715
    v2 = v * v
    t = jnp.tanh(a * v * (1.0 + b * v2))
    half = 0.5 * (1.0 + t)
    slope = half + 0.5 * v * (1.0 - t * t) * (a * (1.0 + 3.0 * b * v2))
    return v * half, slope


def place(block, core):
    side = jnp.where(block // HALF == core, 0, 1)
    return side, pl.ds(pl.multiple_of((block % HALF) * BLK, BLK), BLK)


def load_rows(pieces, tok, grad, sem):
    copies = []
    for side in range(2):
        for rel in range(8):
            for which, dst in enumerate((tok, grad)):
                copies.append(
                    pltpu.make_async_copy(
                        pieces[side][rel][which],
                        dst.at[side, pl.ds(16 * rel, 16)],
                        sem.at[len(copies)],
                    )
                )
    for cp in copies:
        cp.start()
    return copies


def split_pieces(refs):
    sides = []
    for side in range(2):
        r = refs[9 * side : 9 * side + 9]
        row = [(q.at[0], q.at[1]) for q in r[:4]] + [(r[4], r[5])]
        row += [(q.at[0], q.at[1]) for q in r[6:]]
        sides.append(row)
    return sides


def loop(body):
    def group(i, carry):
        for j in range(GROUP):
            body(i * GROUP + j)
        return carry

    lax.fori_loop(0, CAP // GROUP, group, 0)


def dot(a, b, dims):
    return lax.dot_general(a, b, (dims, ((), ())), preferred_element_type=F32)


def forward_kernel(meta, w1, w2, *refs):
    pieces = split_pieces(refs[:18])
    hid, gp, own, oth = refs[18:22]
    tok, grad, pre, back, acc, sem = refs[22:]
    copies = load_rows(pieces, tok, grad, sem)
    pre[...] = jnp.zeros_like(pre)
    back[...] = jnp.zeros_like(back)
    core = meta[CORE]
    n1 = meta[LIVE1]
    n2 = meta[LIVE2]
    for cp in copies:
        cp.wait()

    def up(s):
        side, lanes = place(meta[R1 + s], core)
        col = jnp.where(s < n1, meta[C1 + s], SB)
        pre[col] += dot(tok[side, :, lanes], w1[s], ((1,), (0,)))

    loop(up)

    def down(s):
        side, lanes = place(meta[C2 + s], core)
        row = jnp.where(s < n2, meta[R2 + s], SB)
        back[row] += dot(grad[side, :, lanes], w2[s], ((1,), (1,)))

    loop(down)
    for k in range(SB):
        h, slope = gelu_pair(pre[k])
        hid[k] = h.astype(BF16)
        gp[k] = (back[k] * slope).astype(BF16)

    def finish(which):
        for b in range(HALF):
            own[which, :, b * BLK : (b + 1) * BLK] = acc[core * HALF + b].astype(BF16)
            oth[which, :, b * BLK : (b + 1) * BLK] = acc[(1 - core) * HALF + b].astype(BF16)

    acc[...] = jnp.zeros_like(acc)

    def out(s):
        col = jnp.where(s < n2, meta[C2 + s], 2 * HALF)
        acc[col] += dot(hid[meta[R2 + s]], w2[s], ((1,), (0,)))

    loop(out)
    finish(0)
    acc[...] = jnp.zeros_like(acc)

    def tback(s):
        row = jnp.where(s < n1, meta[R1 + s], 2 * HALF)
        acc[row] += dot(gp[meta[C1 + s]], w1[s], ((1,), (1,)))

    loop(tback)
    finish(1)


def weight_kernel(meta, hid, gp, *refs):
    pieces = split_pieces(refs[:18])
    o2 = refs[18:22]
    o1 = refs[22:24]
    tok, grad, d2, d1, sem, osem = refs[24:]
    copies = load_rows(pieces, tok, grad, sem)
    core = meta[CORE]
    px = meta[PX]
    pyh = meta[PYH]
    n1 = meta[LIVE1]
    n2 = meta[LIVE2]
    for cp in copies:
        cp.wait()

    def second(s):
        side, lanes = place(meta[C2 + s], core)
        v = dot(hid[meta[R2 + s]], grad[side, :, lanes], ((0,), (0,)))
        v = jnp.where(s < n2, v, 0.0).astype(BF16)
        for j in range(8):
            d2[(j % 4 - px) & 3, (j // 4) ^ pyh, s] = v[16 * j : 16 * j + 16]

    loop(second)

    def first(s):
        side, lanes = place(meta[R1 + s], core)
        v = dot(tok[side, :, lanes], gp[meta[C1 + s]], ((0,), (0,)))
        v = jnp.where(s < n1, v, 0.0).astype(BF16)
        for j in range(8):
            d1[(j // 4) ^ pyh, (j % 4 - px) & 3, s] = v[16 * j : 16 * j + 16]

    loop(first)
    outs = [pltpu.make_async_copy(d2.at[k], o2[k], osem.at[k]) for k in range(4)]
    outs += [pltpu.make_async_copy(d1.at[k], o1[k], osem.at[4 + k]) for k in range(2)]
    for cp in outs:
        cp.start()
    for cp in outs:
        cp.wait()


VMEM = pl.BlockSpec(memory_space=pltpu.VMEM)
SMEM = pl.BlockSpec(memory_space=pltpu.SMEM)
ANY = pl.BlockSpec(memory_space=pl.ANY)
LIMIT = 48 * 1024 * 1024


def run_forward(meta, w1, w2, pieces):
    sd = jax.ShapeDtypeStruct
    return pl.pallas_call(
        forward_kernel,
        out_shape=[
            sd((SB, BLK, BLK), BF16),
            sd((SB, BLK, BLK), BF16),
            sd((2, BLK, HALF * BLK), BF16),
            sd((2, BLK, HALF * BLK), BF16),
        ],
        in_specs=[SMEM, VMEM, VMEM] + [ANY] * 18,
        out_specs=[VMEM] * 4,
        scratch_shapes=[
            pltpu.VMEM((2, BLK, HALF * BLK), BF16),
            pltpu.VMEM((2, BLK, HALF * BLK), BF16),
            pltpu.VMEM((SB + 1, BLK, BLK), F32),
            pltpu.VMEM((SB + 1, BLK, BLK), F32),
            pltpu.VMEM((2 * HALF + 1, BLK, BLK), F32),
            pltpu.SemaphoreType.DMA((32,)),
        ],
        compiler_params=pltpu.CompilerParams(vmem_limit_bytes=LIMIT),
        cost_estimate=pl.CostEstimate(flops=1 << 32, bytes_accessed=12 << 20, transcendentals=1 << 16),
    )(meta, w1, w2, *pieces)


def run_weight(meta, hid, gp, pieces):
    sd = jax.ShapeDtypeStruct
    return pl.pallas_call(
        weight_kernel,
        out_shape=[sd((2, CAP, 16, BLK), BF16)] * 4 + [sd((4, CAP, 16, BLK), BF16)] * 2,
        in_specs=[SMEM, VMEM, VMEM] + [ANY] * 18,
        out_specs=[ANY] * 6,
        scratch_shapes=[
            pltpu.VMEM((2, BLK, HALF * BLK), BF16),
            pltpu.VMEM((2, BLK, HALF * BLK), BF16),
            pltpu.VMEM((4, 2, CAP, 16, BLK), BF16),
            pltpu.VMEM((2, 4, CAP, 16, BLK), BF16),
            pltpu.SemaphoreType.DMA((32,)),
            pltpu.SemaphoreType.DMA((6,)),
        ],
        compiler_params=pltpu.CompilerParams(vmem_limit_bytes=LIMIT),
        cost_estimate=pl.CostEstimate(flops=1 << 31, bytes_accessed=8 << 20, transcendentals=0),
    )(meta, hid, gp, *pieces)


def shift(n, k):
    return [(i, (i + k) % n) for i in range(n)]


def flip(k):
    return [(i, i ^ k) for i in range(4)]


def f32(v):
    return v.astype(F32)


def gather_rows(tokens, grads):
    c = lax.axis_index("c")
    low = c == 0
    both = jnp.stack([tokens, grads])
    width = both.shape[2] // 2
    mine = jnp.where(low, both[:, :, :width], both[:, :, width:])
    other = jnp.where(low, both[:, :, width:], both[:, :, :width])
    one = lax.ppermute(other, ("yl", "c"), flip(1))
    two = lax.ppermute(mine, ("yl", "c"), flip(2))
    three = lax.ppermute(other, ("yl", "c"), flip(3))
    chunk = jnp.concatenate(
        [
            jnp.where(low, mine, one),
            jnp.where(low, one, mine),
            jnp.where(low, two, three),
            jnp.where(low, three, two),
        ],
        axis=1,
    )
    up = [chunk]
    down = [chunk]
    for _ in range(3):
        up.append(lax.ppermute(up[-1], "z", shift(8, 1)))
        down.append(lax.ppermute(down[-1], "z", shift(8, 7)))
    far_t = lax.ppermute(up[-1][0], "z", shift(8, 1))
    far_g = lax.ppermute(down[-1][1], "z", shift(8, 7))
    own = [chunk, down[1], down[2], down[3], far_t, far_g, up[3], up[2], up[1]]
    oth = [lax.ppermute(q, "c", shift(2, 1)) for q in own]
    return own + oth


def reduce_tensor(own, oth):
    got = lax.ppermute(oth, "c", shift(2, 1))
    s = (f32(own) + f32(got)).reshape(2, 8, 16, -1)
    up = lax.ppermute(s[0, 4].astype(BF16), "z", shift(8, 1))
    down = lax.ppermute(s[1, 4].astype(BF16), "z", shift(8, 7))
    u = jnp.stack([s[0, 3] + f32(up), s[1, 3]])
    d = jnp.stack([s[0, 5], s[1, 5] + f32(down)])
    for k in (2, 3):
        up = lax.ppermute(u.astype(BF16), "z", shift(8, 1))
        down = lax.ppermute(d.astype(BF16), "z", shift(8, 7))
        u = s[:, 4 - k] + f32(up)
        d = s[:, 4 + k] + f32(down)
    up = lax.ppermute(u.astype(BF16), "z", shift(8, 1))
    down = lax.ppermute(d.astype(BF16), "z", shift(8, 7))
    t = s[:, 0] + f32(up) + f32(down)
    got = lax.ppermute(t[:, 8:].astype(BF16), "yl", shift(2, 1))
    t = (t[:, :8] + f32(got)).astype(BF16)
    low = lax.axis_index("c") == 0
    mine = jnp.where(low, t[:, :4], t[:, 4:])
    got = lax.ppermute(jnp.where(low, t[:, 4:], t[:, :4]), "c", shift(2, 1))
    both = jnp.concatenate([jnp.where(low, mine, got), jnp.where(low, got, mine)], axis=2)
    return both[0], both[1]


def reduce_x_first(parts):
    got = [lax.ppermute(parts[k], "x", shift(4, k)) for k in (1, 2, 3)]
    s = f32(parts[0]) + f32(got[0]) + f32(got[1]) + f32(got[2])
    far = lax.ppermute(s[1].astype(BF16), "yh", shift(2, 1))
    return s[0] + f32(far)


def reduce_y_first(parts):
    far = lax.ppermute(parts[1], "yh", shift(2, 1))
    s = f32(parts[0]) + f32(far)
    got = [lax.ppermute(s[k].astype(BF16), "x", shift(4, k)) for k in (1, 2, 3)]
    return s[0] + f32(got[0]) + f32(got[1]) + f32(got[2])


def shards(tokens, grads, w1, w1_rows, w1_cols, w1_count, w2, w2_rows, w2_cols, w2_count):
    stripe = (lax.axis_index("z") * 2 + lax.axis_index("yl")) * 2 + lax.axis_index("c")
    here = jnp.stack([lax.axis_index("c"), lax.axis_index("x"), lax.axis_index("yh")])
    meta = jnp.concatenate(
        [
            w1_rows,
            w1_cols - stripe * SB,
            w2_rows - stripe * SB,
            w2_cols,
            w1_count,
            w2_count,
            here.astype(jnp.int32),
        ]
    )
    pieces = gather_rows(tokens, grads)
    hid, gp, own, oth = run_forward(meta, w1, w2, pieces)
    parts = run_weight(meta, hid, gp, pieces)
    grad_w2 = reduce_x_first(parts[:4])
    grad_w1 = reduce_y_first(parts[4:])
    layer_out, grad_tokens = reduce_tensor(own, oth)
    return layer_out, grad_tokens, grad_w1, grad_w2


def solution(mesh):
    fine = Mesh(mesh.devices.reshape(SIZES), AXES)
    rows = P(AXES, None)
    stripe = ("z", "yl", "c")
    flat = P(stripe)
    blocks = P(stripe, None, None)
    in_specs = (rows, rows, blocks, flat, flat, flat, blocks, flat, flat, flat)
    grads = P(stripe, ("yh", "x"), None)
    out_specs = (rows, rows, grads, grads)
    return jax.shard_map(
        shards, mesh=fine, in_specs=in_specs, out_specs=out_specs, check_vma=False
    )
```

```python
import jax
import jax.numpy as jnp
from jax import lax
from jax.experimental import pallas as pl
from jax.experimental.pallas import tpu as pltpu
from jax.sharding import Mesh
from jax.sharding import PartitionSpec as P

AXES = ("yh", "x", "z", "yl", "c")
SIZES = (2, 4, 8, 2, 2)
BLK = 128
SB = 4
CAP = 64
DB = 64
WIDTH = DB * BLK
F32 = jnp.float32
BF16 = jnp.bfloat16
GROUP = 32
R1, C1, R2, C2, LIVE1, LIVE2, CORE, PX, PYH = 0, 64, 128, 192, 256, 257, 258, 259, 260
MB = 1024 * 1024


def gelu_pair(v):
    a = 0.7978845608028654
    b = 0.044715
    v2 = v * v
    t = jnp.tanh(a * v * (1.0 + b * v2))
    half = 0.5 * (1.0 + t)
    slope = half + 0.5 * v * (1.0 - t * t) * (a * (1.0 + 3.0 * b * v2))
    return v * half, slope


def lanes(block):
    return pl.ds(pl.multiple_of(block * BLK, BLK), BLK)


def loop(body):
    def group(i, carry):
        for j in range(GROUP):
            body(i * GROUP + j)
        return carry

    lax.fori_loop(0, CAP // GROUP, group, 0)


def dot(a, b, dims):
    return lax.dot_general(a, b, (dims, ((), ())), preferred_element_type=F32)


def join(refs, which, dst):
    for i in range(8):
        low, high = refs[2 * i], refs[2 * i + 1]
        rows = jnp.concatenate([low[which].astype(F32), high[which].astype(F32)], axis=0)
        dst[16 * i : 16 * i + 16] = rows.astype(BF16)


def forward_kernel(meta, w1, w2, *refs):
    pieces = refs[:16]
    hid, gp, tok, grad, own, early, late = refs[16:23]
    pre, back, acc = refs[23:]
    join(pieces, 0, tok)
    join(pieces, 1, grad)
    pre[...] = jnp.zeros_like(pre)
    back[...] = jnp.zeros_like(back)
    n1 = meta[LIVE1]
    n2 = meta[LIVE2]

    def up(s):
        col = jnp.where(s < n1, meta[C1 + s], SB)
        pre[col] += dot(tok[:, lanes(meta[R1 + s])], w1[s], ((1,), (0,)))

    loop(up)

    def down(s):
        row = jnp.where(s < n2, meta[R2 + s], SB)
        back[row] += dot(grad[:, lanes(meta[C2 + s])], w2[s], ((1,), (1,)))

    loop(down)
    for k in range(SB):
        h, slope = gelu_pair(pre[k])
        hid[k] = h.astype(BF16)
        gp[k] = (back[k] * slope).astype(BF16)

    def finish(which):
        for b in range(DB):
            here = slice(b * BLK, (b + 1) * BLK)
            v = acc[b].astype(BF16)
            own[which, :, here] = v[:64]
            early[which, :, here] = v[64:80]
            late[which, :, here] = v[80:]

    acc[...] = jnp.zeros_like(acc)

    def out(s):
        col = jnp.where(s < n2, meta[C2 + s], DB)
        acc[col] += dot(hid[meta[R2 + s]], w2[s], ((1,), (0,)))

    loop(out)
    finish(0)
    acc[...] = jnp.zeros_like(acc)

    def tback(s):
        row = jnp.where(s < n1, meta[R1 + s], DB)
        acc[row] += dot(gp[meta[C1 + s]], w1[s], ((1,), (1,)))

    loop(tback)
    finish(1)


def rel_x(meta, j):
    d = j % 4 - meta[PX]
    return jnp.where(meta[CORE] == 0, d, -d) & 3


def weight1_kernel(meta, gp, tok, near, far):
    n1 = meta[LIVE1]
    pyh = meta[PYH]

    def first(s):
        v = dot(tok[:, lanes(meta[R1 + s])], gp[meta[C1 + s]], ((0,), (0,)))
        v = jnp.where(s < n1, v, 0.0).astype(BF16)
        for j in range(4):
            k = rel_x(meta, j)
            low, high = v[16 * j : 16 * j + 16], v[16 * j + 64 : 16 * j + 80]
            near[k, s] = jnp.where(pyh == 0, low, high)
            far[k, s] = jnp.where(pyh == 0, high, low)

    loop(first)


def weight2_kernel(meta, hid, grad, *outs):
    n2 = meta[LIVE2]
    pyh = meta[PYH]
    stage = outs[4]

    def second(s):
        v = dot(hid[meta[R2 + s]], grad[:, lanes(meta[C2 + s])], ((0,), (0,)))
        v = jnp.where(s < n2, v, 0.0).astype(BF16)
        for j in range(8):
            stage[rel_x(meta, j), (j // 4) ^ pyh, s] = v[16 * j : 16 * j + 16]

    loop(second)
    sem = outs[5]
    copies = [pltpu.make_async_copy(stage.at[k], outs[k], sem.at[k]) for k in range(4)]
    for cp in copies:
        cp.start()
    for cp in copies:
        cp.wait()


VMEM = pl.BlockSpec(memory_space=pltpu.VMEM)
SMEM = pl.BlockSpec(memory_space=pltpu.SMEM)
ANY = pl.BlockSpec(memory_space=pl.ANY)


def run_forward(meta, w1, w2, pieces):
    sd = jax.ShapeDtypeStruct
    return pl.pallas_call(
        forward_kernel,
        out_shape=[
            sd((SB, BLK, BLK), BF16),
            sd((SB, BLK, BLK), BF16),
            sd((BLK, WIDTH), BF16),
            sd((BLK, WIDTH), BF16),
            sd((2, 64, WIDTH), BF16),
            sd((2, 16, WIDTH), BF16),
            sd((2, 48, WIDTH), BF16),
        ],
        in_specs=[SMEM, VMEM, VMEM] + [VMEM] * 16,
        out_specs=[VMEM] * 7,
        scratch_shapes=[
            pltpu.VMEM((SB + 1, BLK, BLK), F32),
            pltpu.VMEM((SB + 1, BLK, BLK), F32),
            pltpu.VMEM((DB + 1, BLK, BLK), F32),
        ],
        compiler_params=pltpu.CompilerParams(vmem_limit_bytes=32 * MB),
        cost_estimate=pl.CostEstimate(flops=1 << 32, bytes_accessed=12 * MB, transcendentals=1 << 16),
        name="forward",
    )(meta, w1, w2, *pieces)


def run_weight1(meta, gp, tok):
    sd = jax.ShapeDtypeStruct
    return pl.pallas_call(
        weight1_kernel,
        out_shape=[sd((4, CAP, 16, BLK), BF16)] * 2,
        in_specs=[SMEM, VMEM, VMEM],
        out_specs=[VMEM] * 2,
        compiler_params=pltpu.CompilerParams(vmem_limit_bytes=16 * MB),
        cost_estimate=pl.CostEstimate(flops=1 << 30, bytes_accessed=4 * MB, transcendentals=0),
        name="weight1",
    )(meta, gp, tok)


def run_weight2(meta, hid, grad):
    sd = jax.ShapeDtypeStruct
    return pl.pallas_call(
        weight2_kernel,
        out_shape=[sd((2, CAP, 16, BLK), BF16)] * 4,
        in_specs=[SMEM, VMEM, VMEM],
        out_specs=[ANY] * 4,
        scratch_shapes=[pltpu.VMEM((4, 2, CAP, 16, BLK), BF16), pltpu.SemaphoreType.DMA((4,))],
        compiler_params=pltpu.CompilerParams(vmem_limit_bytes=16 * MB),
        cost_estimate=pl.CostEstimate(flops=1 << 30, bytes_accessed=4 * MB, transcendentals=0),
        name="weight2",
    )(meta, hid, grad)


def swap(v, axis):
    return lax.ppermute(v, axis, [(0, 1), (1, 0)])


def ring(v, axis, n, sign):
    pairs = []
    for i in range(n):
        for c in range(2):
            step = sign if c == 0 else -sign
            pairs.append((i * 2 + c, ((i + step) % n) * 2 + c))
    if axis == "z":
        full = []
        for i in range(n):
            for y in range(2):
                for c in range(2):
                    step = sign if c == 0 else -sign
                    full.append(((i * 2 + y) * 2 + c, (((i + step) % n) * 2 + y) * 2 + c))
        return lax.ppermute(v, ("z", "yl", "c"), full)
    return lax.ppermute(v, (axis, "c"), pairs)


def f32(v):
    return v.astype(F32)


def narrow(v):
    return v.astype(BF16)


def gather_rows(tokens, grads):
    more_t = swap(tokens, "yl")
    more_g = swap(grads, "yl")
    chunk = jnp.stack([jnp.concatenate([tokens, more_t], 0), jnp.concatenate([grads, more_g], 0)])
    a = [chunk]
    b = [chunk]
    for _ in range(3):
        a.append(ring(a[-1], "z", 8, 1))
        b.append(ring(b[-1], "z", 8, -1))
    a.append(ring(a[-1], "z", 8, 1))
    own = [a[4], a[3], b[3], a[2], b[2], a[1], b[1], a[0]]
    arrival = [7, 5, 6, 3, 4, 1, 2, 0]
    oth = {i: swap(own[i], "c") for i in arrival}
    return own + [oth[i] for i in range(8)]


def reduce_tensor(own, early, late):
    got_early = swap(early, "c")
    got_late = swap(late, "c")

    def part(i):
        mine = f32(own[:, 8 * i : 8 * i + 8])
        if i < 2:
            return mine + f32(got_early[:, 8 * i : 8 * i + 8])
        return mine + f32(got_late[:, 8 * i - 16 : 8 * i - 8])

    a = ring(narrow(part(0)), "z", 8, 1)
    b = ring(narrow(part(1)), "z", 8, -1)
    a = ring(narrow(part(2) + f32(a)), "z", 8, 1)
    b = ring(narrow(part(3) + f32(b)), "z", 8, -1)
    a = ring(narrow(part(4) + f32(a)), "z", 8, 1)
    b = ring(narrow(part(5) + f32(b)), "z", 8, -1)
    a = ring(narrow(part(6) + f32(a)), "z", 8, 1)
    t = part(7) + f32(a) + f32(b)
    got = swap(narrow(t[:, 4:]), "yl")
    t = narrow(t[:, :4] + f32(got))
    return t[0], t[1]


def ring_x(parts):
    a = ring(narrow(parts[2]), "x", 4, 1)
    b = ring(narrow(parts[3]), "x", 4, -1)
    a = ring(narrow(f32(parts[1]) + f32(a)), "x", 4, 1)
    return f32(parts[0]) + f32(a) + f32(b)


def reduce_x_first(parts):
    s = ring_x(parts)
    far = swap(narrow(s[1]), "yh")
    return s[0] + f32(far)


def reduce_y_first(near, far):
    got = swap(far, "yh")
    return ring_x([f32(near[k]) + f32(got[k]) for k in range(4)])


def shards(tokens, grads, w1, w1_rows, w1_cols, w1_count, w2, w2_rows, w2_cols, w2_count):
    stripe = (lax.axis_index("z") * 2 + lax.axis_index("yl")) * 2 + lax.axis_index("c")
    here = jnp.stack([lax.axis_index("c"), lax.axis_index("x"), lax.axis_index("yh")])
    meta = jnp.concatenate(
        [
            w1_rows,
            w1_cols - stripe * SB,
            w2_rows - stripe * SB,
            w2_cols,
            w1_count,
            w2_count,
            here.astype(jnp.int32),
        ]
    )
    pieces = gather_rows(tokens, grads)
    hid, gp, tok, grad, own, early, late = run_forward(meta, w1, w2, pieces)
    near, far = run_weight1(meta, gp, tok)
    parts = run_weight2(meta, hid, grad)
    grad_w1 = reduce_y_first(near, far)
    grad_w2 = reduce_x_first(parts)
    layer_out, grad_tokens = reduce_tensor(own, early, late)
    return layer_out, grad_tokens, grad_w1, grad_w2


def solution(mesh):
    fine = Mesh(mesh.devices.reshape(SIZES), AXES)
    rows = P(AXES, None)
    stripe = ("z", "yl", "c")
    flat = P(stripe)
    blocks = P(stripe, None, None)
    in_specs = (rows, rows, blocks, flat, flat, flat, blocks, flat, flat, flat)
    grads = P(stripe, ("yh", "x"), None)
    out_specs = (rows, rows, grads, grads)
    return jax.shard_map(
        shards, mesh=fine, in_specs=in_specs, out_specs=out_specs, check_vma=False
    )
```

```python
import jax
import jax.numpy as jnp
from jax import lax
from jax.experimental import pallas as pl
from jax.experimental.pallas import tpu as pltpu
from jax.sharding import Mesh
from jax.sharding import PartitionSpec as P

AXES = ("yh", "x", "z", "yl", "c")
SIZES = (2, 4, 8, 2, 2)
BLK = 128
SB = 4
CAP = 64
DB = 64
WIDTH = DB * BLK
F32 = jnp.float32
BF16 = jnp.bfloat16
GROUP = 32
R1, C1, R2, C2, LIVE1, LIVE2, CORE, PX, PYH = 0, 64, 128, 192, 256, 257, 258, 259, 260
MB = 1024 * 1024


def gelu_pair(v):
    a = 0.7978845608028654
    b = 0.044715
    v2 = v * v
    t = jnp.tanh(a * v * (1.0 + b * v2))
    half = 0.5 * (1.0 + t)
    slope = half + 0.5 * v * (1.0 - t * t) * (a * (1.0 + 3.0 * b * v2))
    return v * half, slope


def lanes(block):
    return pl.ds(pl.multiple_of(block * BLK, BLK), BLK)


def loop(body):
    def group(i, carry):
        for j in range(GROUP):
            body(i * GROUP + j)
        return carry

    lax.fori_loop(0, CAP // GROUP, group, 0)


def dot(a, b, dims):
    return lax.dot_general(a, b, (dims, ((), ())), preferred_element_type=F32)


def join(refs, which, dst):
    for i in range(8):
        low, high = refs[2 * i], refs[2 * i + 1]
        rows = jnp.concatenate([low[which].astype(F32), high[which].astype(F32)], axis=0)
        dst[16 * i : 16 * i + 16] = rows.astype(BF16)


def hidden_kernel(meta, w1, w2, *refs):
    pieces = refs[:16]
    hid, gp, tok, grad, pre, back = refs[16:]
    join(pieces, 0, tok)
    join(pieces, 1, grad)
    pre[...] = jnp.zeros_like(pre)
    back[...] = jnp.zeros_like(back)

    def up(s):
        pre[meta[C1 + s]] += dot(tok[:, lanes(meta[R1 + s])], w1[s], ((1,), (0,)))

    loop(up)

    def down(s):
        back[meta[R2 + s]] += dot(grad[:, lanes(meta[C2 + s])], w2[s], ((1,), (1,)))

    loop(down)
    for k in range(SB):
        h, slope = gelu_pair(pre[k])
        hid[k] = h.astype(BF16)
        gp[k] = (back[k] * slope).astype(BF16)


def partial_kernel(meta, w1, w2, hid, gp, own, other, acc):
    def finish(which):
        for b in range(DB):
            here = slice(b * BLK, (b + 1) * BLK)
            v = acc[b]
            own[which, :, here] = v[:64].astype(BF16)
            other[which, :, here] = v[64:].astype(BF16)

    acc[...] = jnp.zeros_like(acc)

    def out(s):
        acc[meta[C2 + s]] += dot(hid[meta[R2 + s]], w2[s], ((1,), (0,)))

    loop(out)
    finish(0)
    acc[...] = jnp.zeros_like(acc)

    def tback(s):
        acc[meta[R1 + s]] += dot(gp[meta[C1 + s]], w1[s], ((1,), (1,)))

    loop(tback)
    finish(1)


def rel_x(meta, j):
    d = j % 4 - meta[PX]
    return jnp.where(meta[CORE] == 0, d, -d) & 3


def weight1_kernel(meta, gp, tok, near, far):
    n1 = meta[LIVE1]
    pyh = meta[PYH]

    def first(s):
        v = dot(tok[:, lanes(meta[R1 + s])], gp[meta[C1 + s]], ((0,), (0,)))
        v = jnp.where(s < n1, v, 0.0).astype(BF16)
        for j in range(4):
            k = rel_x(meta, j)
            low, high = v[16 * j : 16 * j + 16], v[16 * j + 64 : 16 * j + 80]
            near[k, s] = jnp.where(pyh == 0, low, high)
            far[k, s] = jnp.where(pyh == 0, high, low)

    loop(first)


def weight2_kernel(meta, hid, grad, *outs):
    n2 = meta[LIVE2]
    pyh = meta[PYH]
    stage = outs[4]

    def second(s):
        v = dot(hid[meta[R2 + s]], grad[:, lanes(meta[C2 + s])], ((0,), (0,)))
        v = jnp.where(s < n2, v, 0.0).astype(BF16)
        for j in range(8):
            stage[rel_x(meta, j), (j // 4) ^ pyh, s] = v[16 * j : 16 * j + 16]

    loop(second)
    sem = outs[5]
    copies = [pltpu.make_async_copy(stage.at[k], outs[k], sem.at[k]) for k in range(4)]
    for cp in copies:
        cp.start()
    for cp in copies:
        cp.wait()


VMEM = pl.BlockSpec(memory_space=pltpu.VMEM)
SMEM = pl.BlockSpec(memory_space=pltpu.SMEM)
ANY = pl.BlockSpec(memory_space=pl.ANY)


def sds(*shape):
    return jax.ShapeDtypeStruct(shape, BF16)


def run_hidden(meta, w1, w2, pieces):
    return pl.pallas_call(
        hidden_kernel,
        out_shape=[sds(SB, BLK, BLK)] * 2 + [sds(BLK, WIDTH)] * 2,
        in_specs=[SMEM, VMEM, VMEM] + [VMEM] * 16,
        out_specs=[VMEM] * 4,
        scratch_shapes=[pltpu.VMEM((SB, BLK, BLK), F32)] * 2,
        compiler_params=pltpu.CompilerParams(vmem_limit_bytes=24 * MB),
        cost_estimate=pl.CostEstimate(flops=1 << 31, bytes_accessed=12 * MB, transcendentals=1 << 16),
        name="hidden",
    )(meta, w1, w2, *pieces)


def run_partial(meta, w1, w2, hid, gp):
    return pl.pallas_call(
        partial_kernel,
        out_shape=[sds(2, 64, WIDTH)] * 2,
        in_specs=[SMEM] + [VMEM] * 4,
        out_specs=[VMEM] * 2,
        scratch_shapes=[pltpu.VMEM((DB, BLK, BLK), F32)],
        compiler_params=pltpu.CompilerParams(vmem_limit_bytes=24 * MB),
        cost_estimate=pl.CostEstimate(flops=1 << 31, bytes_accessed=12 * MB, transcendentals=0),
        name="partial",
    )(meta, w1, w2, hid, gp)


def run_weight1(meta, gp, tok):
    sd = jax.ShapeDtypeStruct
    return pl.pallas_call(
        weight1_kernel,
        out_shape=[sd((4, CAP, 16, BLK), BF16)] * 2,
        in_specs=[SMEM, VMEM, VMEM],
        out_specs=[VMEM] * 2,
        compiler_params=pltpu.CompilerParams(vmem_limit_bytes=16 * MB),
        cost_estimate=pl.CostEstimate(flops=1 << 30, bytes_accessed=4 * MB, transcendentals=0),
        name="weight1",
    )(meta, gp, tok)


def run_weight2(meta, hid, grad):
    sd = jax.ShapeDtypeStruct
    return pl.pallas_call(
        weight2_kernel,
        out_shape=[sd((2, CAP, 16, BLK), BF16)] * 4,
        in_specs=[SMEM, VMEM, VMEM],
        out_specs=[ANY] * 4,
        scratch_shapes=[pltpu.VMEM((4, 2, CAP, 16, BLK), BF16), pltpu.SemaphoreType.DMA((4,))],
        compiler_params=pltpu.CompilerParams(vmem_limit_bytes=16 * MB),
        cost_estimate=pl.CostEstimate(flops=1 << 30, bytes_accessed=4 * MB, transcendentals=0),
        name="weight2",
    )(meta, hid, grad)


def swap(v, axis):
    return lax.ppermute(v, axis, [(0, 1), (1, 0)])


def ring(v, axis, n, sign):
    pairs = []
    for i in range(n):
        for c in range(2):
            step = sign if c == 0 else -sign
            pairs.append((i * 2 + c, ((i + step) % n) * 2 + c))
    if axis == "z":
        full = []
        for i in range(n):
            for y in range(2):
                for c in range(2):
                    step = sign if c == 0 else -sign
                    full.append(((i * 2 + y) * 2 + c, (((i + step) % n) * 2 + y) * 2 + c))
        return lax.ppermute(v, ("z", "yl", "c"), full)
    return lax.ppermute(v, (axis, "c"), pairs)


def f32(v):
    return v.astype(F32)


def narrow(v):
    return v.astype(BF16)


def tie(*values):
    return lax.optimization_barrier(values)


def gather_rows(tokens, grads, early):
    more_t = swap(tokens, "yl")
    more_g = swap(grads, "yl")
    chunk = jnp.stack([jnp.concatenate([tokens, more_t], 0), jnp.concatenate([grads, more_g], 0)])
    early = prepare(*tie(chunk, *early)[1:])
    later, *early = tie(chunk, *early)
    a = [chunk]
    b = [later]
    for _ in range(3):
        a.append(ring(a[-1], "z", 8, 1))
        b.append(ring(b[-1], "z", 8, -1))
    a.append(ring(a[-1], "z", 8, 1))
    own = [a[4], a[3], b[3], a[2], b[2], a[1], b[1], a[0]]
    return own + [swap(v, "c") for v in own], early


def reduce_all(own, other, near, far, parts):
    def part(i):
        here = slice(8 * i, 8 * i + 8)
        return f32(own[:, here]) + f32(other[:, here])

    across1 = swap(far, "yh")
    za = ring(narrow(part(0)), "z", 8, 1)
    zb = ring(narrow(part(1)), "z", 8, -1)
    xa = ring(parts[2], "x", 4, 1)
    xb = ring(parts[3], "x", 4, -1)

    za, zb = tie(za, zb)
    za, zb = tie(narrow(part(2) + f32(za)), narrow(part(3) + f32(zb)))
    last = za
    za = ring(za, "z", 8, 1)
    zb = ring(zb, "z", 8, -1)

    xa, xb, last = tie(xa, xb, last)
    last = narrow(f32(parts[1]) + f32(xa))
    xa = ring(last, "x", 4, 1)

    za, zb, last = tie(za, zb, last)
    za, zb = tie(narrow(part(4) + f32(za)), narrow(part(5) + f32(zb)))
    last = za
    za = ring(za, "z", 8, 1)
    zb = ring(zb, "z", 8, -1)

    across1, last = tie(across1, last)
    w1 = [f32(near[k]) + f32(across1[k]) for k in range(4)]
    xc, xd = tie(narrow(w1[2]), narrow(w1[3]))
    last = xc
    xc = ring(xc, "x", 4, 1)
    xd = ring(xd, "x", 4, -1)

    xa, last = tie(xa, last)
    half = f32(parts[0]) + f32(xa) + f32(xb)
    last = narrow(half[1])
    across2 = swap(last, "yh")

    za, zb, last = tie(za, zb, last)
    last = narrow(part(6) + f32(za))
    za = ring(last, "z", 8, 1)

    xc, xd, last = tie(xc, xd, last)
    last = narrow(w1[1] + f32(xc))
    xc = ring(last, "x", 4, 1)

    za, last = tie(za, last)
    t = part(7) + f32(za) + f32(zb)
    last = narrow(t[:, 4:])
    got = swap(last, "yl")

    across2, last = tie(across2, last)
    grad_w2 = half[0] + f32(across2)
    xc, grad_w2 = tie(xc, grad_w2)
    grad_w1 = w1[0] + f32(xc) + f32(xd)
    t = narrow(t[:, :4] + f32(got))
    return t[0], t[1], grad_w1, grad_w2


def prepare(w1, w2, w1_rows, w1_cols, w1_count, w2_rows, w2_cols, w2_count):
    stripe = (lax.axis_index("z") * 2 + lax.axis_index("yl")) * 2 + lax.axis_index("c")
    here = jnp.stack([lax.axis_index("c"), lax.axis_index("x"), lax.axis_index("yh")])
    meta = jnp.concatenate(
        [
            w1_rows,
            jnp.clip(w1_cols - stripe * SB, 0, SB - 1),
            jnp.clip(w2_rows - stripe * SB, 0, SB - 1),
            w2_cols,
            w1_count,
            w2_count,
            here.astype(jnp.int32),
        ]
    )
    slot = jnp.arange(CAP, dtype=jnp.int32)[:, None, None]
    live1 = jnp.where(slot < w1_count[0], w1, jnp.zeros_like(w1))
    live2 = jnp.where(slot < w2_count[0], w2, jnp.zeros_like(w2))
    return live1, live2, meta


def shards(tokens, grads, w1, w1_rows, w1_cols, w1_count, w2, w2_rows, w2_cols, w2_count):
    early = (w1, w2, w1_rows, w1_cols, w1_count, w2_rows, w2_cols, w2_count)
    pieces, (live1, live2, meta) = gather_rows(tokens, grads, early)
    hid, gp, tok, grad = run_hidden(meta, live1, live2, pieces)
    own, other = run_partial(meta, live1, live2, hid, gp)
    gp, other = tie(gp, other)
    other = swap(other, "c")
    near, far = run_weight1(meta, gp, tok)
    hid, near = tie(hid, near)
    parts = run_weight2(meta, hid, grad)
    other, *parts = tie(other, *parts)
    layer_out, grad_tokens, grad_w1, grad_w2 = reduce_all(own, other, near, far, parts)
    return layer_out, grad_tokens, grad_w1, grad_w2


def solution(mesh):
    fine = Mesh(mesh.devices.reshape(SIZES), AXES)
    rows = P(AXES, None)
    stripe = ("z", "yl", "c")
    flat = P(stripe)
    blocks = P(stripe, None, None)
    in_specs = (rows, rows, blocks, flat, flat, flat, blocks, flat, flat, flat)
    grads = P(stripe, ("yh", "x"), None)
    out_specs = (rows, rows, grads, grads)
    return jax.shard_map(
        shards, mesh=fine, in_specs=in_specs, out_specs=out_specs, check_vma=False
    )
```

```python
import jax
import jax.numpy as jnp
from jax import lax
from jax.experimental import pallas as pl
from jax.experimental.pallas import tpu as pltpu
from jax.sharding import Mesh
from jax.sharding import PartitionSpec as P

AXES = ("yh", "x", "z", "yl", "c")
SIZES = (2, 4, 8, 2, 2)
BLK = 128
SB = 4
CAP = 64
DB = 64
WIDTH = DB * BLK
F32 = jnp.float32
BF16 = jnp.bfloat16
FEW = 0
R1, C1, R2, C2, LIVE1, LIVE2, CORE, PX, PYH = 0, 64, 128, 192, 256, 257, 258, 259, 260
MB = 1024 * 1024


def gelu_pair(v):
    a = 0.7978845608028654
    b = 0.044715
    v2 = v * v
    t = jnp.tanh(a * v * (1.0 + b * v2))
    half = 0.5 * (1.0 + t)
    slope = half + 0.5 * v * (1.0 - t * t) * (a * (1.0 + 3.0 * b * v2))
    return v * half, slope


def lanes(block):
    return pl.ds(pl.multiple_of(block * BLK, BLK), BLK)


def loop(body, start=0, group=64):
    def step(i, carry):
        for j in range(group):
            body(start + i * group + j)
        return carry

    lax.fori_loop(0, (CAP - start) // group, step, 0)


def dot(a, b, dims):
    return lax.dot_general(a, b, (dims, ((), ())), preferred_element_type=F32)


def hidden_kernel(meta, w1, w2, *refs):
    p, q, pm, qm = refs[:5], refs[5:9], refs[9:13], refs[13:16]
    hid, gp, tok, grad, pre, back = refs[16:]
    low = meta[CORE] == 0

    def put(unit, a, b):
        rows = slice(16 * unit, 16 * unit + 16)
        a, b = a[...], b[...]
        tok[rows] = jnp.where(low, a, b)
        grad[rows] = jnp.where(low, b, a)

    put(0, p[4], pm[3])
    for i, k in enumerate((3, 2, 1)):
        put(1 + i, p[k], q[k])
        put(4 + i, qm[k - 1], pm[k - 1])
    put(7, p[0], q[0])
    pre[...] = jnp.zeros_like(pre)
    back[...] = jnp.zeros_like(back)

    def up(s):
        pre[meta[C1 + s]] += dot(tok[:, lanes(meta[R1 + s])], w1[s], ((1,), (0,)))

    loop(up)

    def down(s):
        back[meta[R2 + s]] += dot(grad[:, lanes(meta[C2 + s])], w2[s], ((1,), (1,)))

    loop(down)
    for k in range(SB):
        h, slope = gelu_pair(pre[k])
        hid[k] = h.astype(BF16)
        gp[k] = (back[k] * slope).astype(BF16)


def partial_kernel(meta, w1, w2, hid, gp, after, far, send_far, near, send, acc):
    core = meta[CORE]

    def finish(stream):
        for b in range(DB):
            here = slice(b * BLK, (b + 1) * BLK)
            v = acc[b].astype(BF16)
            if stream == 0:
                far[:, here] = v[:16]
            else:
                send_far[:, here] = v[:16]
            send[1 - stream, :, here] = v[16:64]
            near[stream, :, here] = v[64:]

    def finish_array(which):
        pl.when(core == which)(lambda: finish(0))
        pl.when(core != which)(lambda: finish(1))

    acc[...] = jnp.zeros_like(acc)

    def out(s):
        acc[meta[C2 + s]] += dot(hid[meta[R2 + s]], w2[s], ((1,), (0,)))

    loop(out)
    finish_array(0)
    acc[...] = jnp.zeros_like(acc)

    def tback(s):
        acc[meta[R1 + s]] += dot(gp[meta[C1 + s]], w1[s], ((1,), (1,)))

    loop(tback)
    finish_array(1)


def rel_x(meta, j):
    d = j % 4 - meta[PX]
    return jnp.where(meta[CORE] == 0, d, -d) & 3


def weight_kernel(meta, hid, gp, tok, grad, near, far, *refs):
    outs, stage, sem = refs[:4], refs[4], refs[5]
    n1 = meta[LIVE1]
    n2 = meta[LIVE2]
    pyh = meta[PYH]

    def put(slot, v):
        for j in range(8):
            stage[rel_x(meta, j), (j // 4) ^ pyh, slot] = v[16 * j : 16 * j + 16]

    def second(s):
        v = dot(hid[meta[R2 + s]], grad[:, lanes(meta[C2 + s])], ((0,), (0,)))
        put(s, jnp.where(s < n2, v, 0.0).astype(BF16))

    def first(s):
        v = dot(tok[:, lanes(meta[R1 + s])], gp[meta[C1 + s]], ((0,), (0,)))
        return jnp.where(s < n1, v, 0.0).astype(BF16)

    loop(second)
    for s in range(FEW):
        put(CAP + s, first(s))
    copies = [pltpu.make_async_copy(stage.at[k], outs[k], sem.at[k]) for k in range(4)]
    for cp in copies:
        cp.start()

    def rest(s):
        v = first(s)
        for j in range(4):
            k = rel_x(meta, j)
            low, high = v[16 * j : 16 * j + 16], v[16 * j + 64 : 16 * j + 80]
            near[k, s - FEW] = jnp.where(pyh == 0, low, high)
            far[k, s - FEW] = jnp.where(pyh == 0, high, low)

    loop(rest, FEW)
    for cp in copies:
        cp.wait()


def chunk_kernel(core, x, xc, y, yc, p, q):
    low = core[0] == 0
    both = []
    for which in range(2):
        rows = []
        for a, b in ((x, xc), (y, yc)):
            a, b = a[which].astype(F32), b[which].astype(F32)
            rows += [jnp.where(low, a, b), jnp.where(low, b, a)]
        both.append(jnp.concatenate(rows, axis=0))
    p[...] = jnp.where(low, both[0], both[1]).astype(BF16)
    q[...] = jnp.where(low, both[1], both[0]).astype(BF16)


VMEM = pl.BlockSpec(memory_space=pltpu.VMEM)
SMEM = pl.BlockSpec(memory_space=pltpu.SMEM)
ANY = pl.BlockSpec(memory_space=pl.ANY)


def sds(*shape):
    return jax.ShapeDtypeStruct(shape, BF16)


def run_hidden(meta, w1, w2, pieces):
    return pl.pallas_call(
        hidden_kernel,
        out_shape=[sds(SB, BLK, BLK)] * 2 + [sds(BLK, WIDTH)] * 2,
        in_specs=[SMEM, VMEM, VMEM] + [VMEM] * 16,
        out_specs=[VMEM] * 4,
        scratch_shapes=[pltpu.VMEM((SB, BLK, BLK), F32)] * 2,
        compiler_params=pltpu.CompilerParams(vmem_limit_bytes=24 * MB),
        cost_estimate=pl.CostEstimate(flops=1 << 31, bytes_accessed=12 * MB, transcendentals=1 << 16),
        name="hidden",
    )(meta, w1, w2, *pieces)


def run_partial(meta, w1, w2, hid, gp, after):
    return pl.pallas_call(
        partial_kernel,
        out_shape=[sds(16, WIDTH)] * 2 + [sds(2, 64, WIDTH), sds(2, 48, WIDTH)],
        in_specs=[SMEM] + [VMEM] * 4 + [ANY],
        out_specs=[VMEM] * 4,
        scratch_shapes=[pltpu.VMEM((DB, BLK, BLK), F32)],
        compiler_params=pltpu.CompilerParams(vmem_limit_bytes=24 * MB),
        cost_estimate=pl.CostEstimate(flops=1 << 31, bytes_accessed=12 * MB, transcendentals=0),
        name="partial",
    )(meta, w1, w2, hid, gp, after)


def run_weight(meta, hid, gp, tok, grad):
    return pl.pallas_call(
        weight_kernel,
        out_shape=[sds(4, CAP - FEW, 16, BLK)] * 2 + [sds(2, CAP + FEW, 16, BLK)] * 4,
        in_specs=[SMEM] + [VMEM] * 4,
        out_specs=[VMEM] * 2 + [ANY] * 4,
        scratch_shapes=[
            pltpu.VMEM((4, 2, CAP + FEW, 16, BLK), BF16),
            pltpu.SemaphoreType.DMA((4,)),
        ],
        compiler_params=pltpu.CompilerParams(vmem_limit_bytes=16 * MB),
        cost_estimate=pl.CostEstimate(flops=1 << 31, bytes_accessed=8 * MB, transcendentals=0),
        name="weight",
    )(meta, hid, gp, tok, grad)


def run_chunk(core, *rows):
    return pl.pallas_call(
        chunk_kernel,
        out_shape=[sds(16, WIDTH)] * 2,
        in_specs=[SMEM] + [VMEM] * 4,
        out_specs=[VMEM] * 2,
        compiler_params=pltpu.CompilerParams(vmem_limit_bytes=8 * MB),
        name="chunk",
    )(core, *rows)


def add(terms, after=(), out=BF16):
    terms = [t if isinstance(t, tuple) else (t, ()) for t in terms]
    count = len(terms)

    def kernel(*refs):
        total = None
        for ref, (_, index) in zip(refs, terms):
            v = (ref[index] if index else ref[...]).astype(F32)
            total = v if total is None else total + v
        refs[-1][...] = total.astype(out)

    shape = jax.eval_shape(lambda a: a[terms[0][1]], terms[0][0]).shape
    return pl.pallas_call(
        kernel,
        out_shape=jax.ShapeDtypeStruct(shape, out),
        in_specs=[VMEM] * count + [ANY] * len(after),
        out_specs=VMEM,
        compiler_params=pltpu.CompilerParams(vmem_limit_bytes=12 * MB),
        cost_estimate=pl.CostEstimate(flops=1, bytes_accessed=MB, transcendentals=0),
        name="add",
    )(*(t[0] for t in terms), *after)


def home_kernel(core, home, p, q, after, away, keep):
    low = core[0] == 0
    p = home[0, 48:].astype(F32) + p[...].astype(F32)
    q = home[1, 48:].astype(F32) + q[...].astype(F32)
    for which, t in enumerate((jnp.where(low, p, q), jnp.where(low, q, p))):
        first = jnp.concatenate([t[0:4], t[8:12]], axis=0)
        second = jnp.concatenate([t[4:8], t[12:16]], axis=0)
        keep[which] = jnp.where(low, first, second)
        away[which] = jnp.where(low, second, first).astype(BF16)


def half_kernel(mine, got, away, keep):
    for which in range(2):
        t = mine[which] + got[which].astype(F32)
        keep[which] = t[:4]
        away[which] = t[4:].astype(BF16)


def run_home(home, p, q, after):
    core = lax.axis_index("c").astype(jnp.int32).reshape(1)
    return pl.pallas_call(
        home_kernel,
        out_shape=[sds(2, 8, WIDTH), jax.ShapeDtypeStruct((2, 8, WIDTH), F32)],
        in_specs=[SMEM] + [VMEM] * 3 + [ANY],
        out_specs=[VMEM] * 2,
        compiler_params=pltpu.CompilerParams(vmem_limit_bytes=12 * MB),
        name="home",
    )(core, home, p, q, after)


def run_half(mine, got):
    return pl.pallas_call(
        half_kernel,
        out_shape=[sds(2, 4, WIDTH), jax.ShapeDtypeStruct((2, 4, WIDTH), F32)],
        in_specs=[VMEM] * 2,
        out_specs=[VMEM] * 2,
        compiler_params=pltpu.CompilerParams(vmem_limit_bytes=12 * MB),
        name="half",
    )(mine, got)


def swap(v, axis):
    return lax.ppermute(v, axis, [(0, 1), (1, 0)])


def ring(v, axis, n, sign):
    pairs = []
    for i in range(n):
        for c in range(2):
            step = sign if c == 0 else -sign
            pairs.append((i * 2 + c, ((i + step) % n) * 2 + c))
    if axis == "z":
        full = []
        for i in range(n):
            for y in range(2):
                for c in range(2):
                    step = sign if c == 0 else -sign
                    full.append(((i * 2 + y) * 2 + c, (((i + step) % n) * 2 + y) * 2 + c))
        return lax.ppermute(v, ("z", "yl", "c"), full)
    return lax.ppermute(v, (axis, "c"), pairs)


def f32(v):
    return v.astype(F32)


def narrow(v):
    return v.astype(BF16)


def tie(*values):
    return lax.optimization_barrier(values)


def gather_rows(tokens, grads, early):
    x = jnp.stack([tokens, grads])
    y = swap(x, "yl")
    core = lax.axis_index("c").astype(jnp.int32).reshape(1)
    p0, q0 = run_chunk(core, x, swap(x, "c"), y, swap(y, "c"))
    w1, w2, count1, count2 = early[0], early[1], early[4], early[7]
    meta = prepare(*tie(p0, *early[2:])[1:])
    p = [p0, ring(p0, "z", 8, 1)]
    q = [q0, ring(q0, "z", 8, 1)]
    p[1], meta = tie(p[1], meta)
    p[1], w1, w2 = tie(p[1], w1, w2)
    slot = jnp.arange(CAP, dtype=jnp.int32)[:, None, None]
    live1 = jnp.where(slot < count1[0], w1, jnp.zeros_like(w1))
    live2 = jnp.where(slot < count2[0], w2, jnp.zeros_like(w2))
    p.append(ring(p[1], "z", 8, 1))
    q.append(ring(q[1], "z", 8, 1))
    p[2], live1, live2 = tie(p[2], live1, live2)
    p.append(ring(p[2], "z", 8, 1))
    q.append(ring(q[2], "z", 8, 1))
    p.append(ring(p[-1], "z", 8, 1))
    return p + q + [swap(v, "c") for v in p[1:]] + [swap(v, "c") for v in q[1:]], (live1, live2, meta)


def reduce_all(far, got_far, near, got, mine1, across1, parts):
    def part(stream, k):
        here = (stream, slice(16 * (3 - k), 16 * (4 - k)))
        return [(near, here), (got, here)]

    op = add([far, got_far])
    p = ring(op, "z", 8, 1)
    op = add(part(1, 3), [op])
    q = ring(op, "z", 8, 1)
    xa = ring(parts[2], "x", 4, 1)
    xb = ring(parts[3], "x", 4, -1)

    op = add([parts[1], xa], [op])
    xa = ring(op, "x", 4, 1)

    op = add(part(0, 3) + [p], [op])
    p = ring(op, "z", 8, 1)
    op = add(part(1, 2) + [q], [op])
    q = ring(op, "z", 8, 1)

    op = add(part(0, 2) + [p], [op])
    p = ring(op, "z", 8, 1)
    op = add(part(1, 1) + [q], [op])
    q = ring(op, "z", 8, 1)

    op = add([(parts[0], (1,)), (xa, (1,)), (xb, (1,))], [op])
    across2 = swap(op, "yh")

    op = add(part(0, 1) + [p], [op])
    p = ring(op, "z", 8, 1)

    op = add([(mine1, (2,)), (across1, (2,))], [op])
    xc = ring(op, "x", 4, 1)
    op = add([(mine1, (3,)), (across1, (3,))], [op])
    xd = ring(op, "x", 4, -1)

    grad_w2 = add([(parts[0], (0,)), (xa, (0,)), (xb, (0,)), across2], [op], F32)
    away, keep = run_home(near, p, q, grad_w2)
    got = swap(away, "c")
    op = add([(mine1, (1,)), (across1, (1,)), xc], [away, xd])
    xc = ring(op, "x", 4, 1)
    away, keep = run_half(keep, got)
    got = swap(away, "yl")
    grad_w1 = add([(mine1, (0,)), (across1, (0,)), xc, xd], [away], F32)
    t = narrow(keep + f32(got))
    return t[0], t[1], grad_w1, grad_w2


def prepare(w1_rows, w1_cols, w1_count, w2_rows, w2_cols, w2_count):
    stripe = (lax.axis_index("z") * 2 + lax.axis_index("yl")) * 2 + lax.axis_index("c")
    here = jnp.stack([lax.axis_index("c"), lax.axis_index("x"), lax.axis_index("yh")])
    meta = jnp.concatenate(
        [
            w1_rows,
            jnp.clip(w1_cols - stripe * SB, 0, SB - 1),
            jnp.clip(w2_rows - stripe * SB, 0, SB - 1),
            w2_cols,
            w1_count,
            w2_count,
            here.astype(jnp.int32),
        ]
    )
    return meta


def shards(tokens, grads, w1, w1_rows, w1_cols, w1_count, w2, w2_rows, w2_cols, w2_count):
    early = (w1, w2, w1_rows, w1_cols, w1_count, w2_rows, w2_cols, w2_count)
    pieces, (live1, live2, meta) = gather_rows(tokens, grads, early)
    hid, gp, tok, grad = run_hidden(meta, live1, live2, pieces)
    mine1, away1, *parts = run_weight(meta, hid, gp, tok, grad)
    far, send_far, near, send = run_partial(meta, live1, live2, hid, gp, mine1)
    got_far = swap(send_far, "c")
    got = swap(send, "c")
    layer_out, grad_tokens, grad_w1, grad_w2 = reduce_all(
        far, got_far, near, got, mine1, swap(away1, "yh"), parts
    )
    return layer_out, grad_tokens, grad_w1, grad_w2


def solution(mesh):
    fine = Mesh(mesh.devices.reshape(SIZES), AXES)
    rows = P(AXES, None)
    stripe = ("z", "yl", "c")
    flat = P(stripe)
    blocks = P(stripe, None, None)
    in_specs = (rows, rows, blocks, flat, flat, flat, blocks, flat, flat, flat)
    grads = P(stripe, ("yh", "x"), None)
    out_specs = (rows, rows, grads, grads)
    return jax.shard_map(
        shards, mesh=fine, in_specs=in_specs, out_specs=out_specs, check_vma=False
    )
```

```python
import jax
import jax.numpy as jnp
from jax import lax
from jax.experimental import pallas as pl
from jax.experimental.pallas import tpu as pltpu
from jax.sharding import Mesh
from jax.sharding import PartitionSpec as P

AXES = ("yh", "x", "z", "yl", "c")
SIZES = (2, 4, 8, 2, 2)
BLK = 128
SB = 4
CAP = 64
DB = 64
WIDTH = DB * BLK
F32 = jnp.float32
BF16 = jnp.bfloat16
FEW = 0
R1, C1, R2, C2, LIVE1, LIVE2, CORE, PX, PYH = 0, 64, 128, 192, 256, 257, 258, 259, 260
MB = 1024 * 1024


def gelu_pair(v):
    a = 0.7978845608028654
    b = 0.044715
    v2 = v * v
    t = jnp.tanh(a * v * (1.0 + b * v2))
    half = 0.5 * (1.0 + t)
    slope = half + 0.5 * v * (1.0 - t * t) * (a * (1.0 + 3.0 * b * v2))
    return v * half, slope


def lanes(block):
    return pl.ds(pl.multiple_of(block * BLK, BLK), BLK)


def loop(body, start=0, group=64):
    def step(i, carry):
        for j in range(group):
            body(start + i * group + j)
        return carry

    lax.fori_loop(0, (CAP - start) // group, step, 0)


def dot(a, b, dims):
    return lax.dot_general(a, b, (dims, ((), ())), preferred_element_type=F32)


def hidden_kernel(meta, w1, w2, *refs):
    p, q, pm, qm = refs[:5], refs[5:9], refs[9:13], refs[13:16]
    hid, gp, tok, grad, pre, back = refs[16:]
    low = meta[CORE] == 0

    def put(unit, a, b):
        rows = slice(16 * unit, 16 * unit + 16)
        a, b = a[...], b[...]
        tok[rows] = jnp.where(low, a, b)
        grad[rows] = jnp.where(low, b, a)

    put(0, p[4], pm[3])
    for i, k in enumerate((3, 2, 1)):
        put(1 + i, p[k], q[k])
        put(4 + i, qm[k - 1], pm[k - 1])
    put(7, p[0], q[0])
    pre[...] = jnp.zeros_like(pre)
    back[...] = jnp.zeros_like(back)

    def up(s):
        pre[meta[C1 + s]] += dot(tok[:, lanes(meta[R1 + s])], w1[s], ((1,), (0,)))

    loop(up)

    def down(s):
        back[meta[R2 + s]] += dot(grad[:, lanes(meta[C2 + s])], w2[s], ((1,), (1,)))

    loop(down)
    for k in range(SB):
        h, slope = gelu_pair(pre[k])
        hid[k] = h.astype(BF16)
        gp[k] = (back[k] * slope).astype(BF16)


def partial_kernel(meta, w1, w2, hid, gp, after, far, send_far, near, send, acc):
    core = meta[CORE]

    def finish(stream):
        for b in range(DB):
            here = slice(b * BLK, (b + 1) * BLK)
            v = acc[b].astype(BF16)
            if stream == 0:
                far[:, here] = v[:16]
            else:
                send_far[:, here] = v[:16]
            send[1 - stream, :, here] = v[16:64]
            near[stream, :, here] = v[64:]

    def finish_array(which):
        pl.when(core == which)(lambda: finish(0))
        pl.when(core != which)(lambda: finish(1))

    acc[...] = jnp.zeros_like(acc)

    def out(s):
        acc[meta[C2 + s]] += dot(hid[meta[R2 + s]], w2[s], ((1,), (0,)))

    loop(out)
    finish_array(0)
    acc[...] = jnp.zeros_like(acc)

    def tback(s):
        acc[meta[R1 + s]] += dot(gp[meta[C1 + s]], w1[s], ((1,), (1,)))

    loop(tback)
    finish_array(1)


def rel_x(meta, j):
    d = j % 4 - meta[PX]
    return jnp.where(meta[CORE] == 0, d, -d) & 3


def weight_kernel(meta, hid, gp, tok, grad, near, far, *refs):
    outs, stage, sem = refs[:4], refs[4], refs[5]
    n1 = meta[LIVE1]
    n2 = meta[LIVE2]
    pyh = meta[PYH]

    def put(slot, v):
        for j in range(8):
            stage[rel_x(meta, j), (j // 4) ^ pyh, slot] = v[16 * j : 16 * j + 16]

    def second(s):
        v = dot(hid[meta[R2 + s]], grad[:, lanes(meta[C2 + s])], ((0,), (0,)))
        put(s, jnp.where(s < n2, v, 0.0).astype(BF16))

    def first(s):
        v = dot(tok[:, lanes(meta[R1 + s])], gp[meta[C1 + s]], ((0,), (0,)))
        return jnp.where(s < n1, v, 0.0).astype(BF16)

    loop(second)
    for s in range(FEW):
        put(CAP + s, first(s))
    copies = [pltpu.make_async_copy(stage.at[k], outs[k], sem.at[k]) for k in range(4)]
    for cp in copies:
        cp.start()

    def rest(s):
        v = first(s)
        for j in range(4):
            k = rel_x(meta, j)
            low, high = v[16 * j : 16 * j + 16], v[16 * j + 64 : 16 * j + 80]
            near[k, s - FEW] = jnp.where(pyh == 0, low, high)
            far[k, s - FEW] = jnp.where(pyh == 0, high, low)

    loop(rest, FEW)
    for cp in copies:
        cp.wait()


def chunk_kernel(core, x, xc, y, yc, p, q):
    low = core[0] == 0
    both = []
    for which in range(2):
        rows = []
        for a, b in ((x, xc), (y, yc)):
            a, b = a[which].astype(F32), b[which].astype(F32)
            rows += [jnp.where(low, a, b), jnp.where(low, b, a)]
        both.append(jnp.concatenate(rows, axis=0))
    p[...] = jnp.where(low, both[0], both[1]).astype(BF16)
    q[...] = jnp.where(low, both[1], both[0]).astype(BF16)


VMEM = pl.BlockSpec(memory_space=pltpu.VMEM)
SMEM = pl.BlockSpec(memory_space=pltpu.SMEM)
ANY = pl.BlockSpec(memory_space=pl.ANY)


def sds(*shape):
    return jax.ShapeDtypeStruct(shape, BF16)


def run_hidden(meta, w1, w2, pieces):
    return pl.pallas_call(
        hidden_kernel,
        out_shape=[sds(SB, BLK, BLK)] * 2 + [sds(BLK, WIDTH)] * 2,
        in_specs=[SMEM, VMEM, VMEM] + [VMEM] * 16,
        out_specs=[VMEM] * 4,
        scratch_shapes=[pltpu.VMEM((SB, BLK, BLK), F32)] * 2,
        compiler_params=pltpu.CompilerParams(vmem_limit_bytes=24 * MB),
        cost_estimate=pl.CostEstimate(flops=1 << 31, bytes_accessed=12 * MB, transcendentals=1 << 16),
        name="hidden",
    )(meta, w1, w2, *pieces)


def run_partial(meta, w1, w2, hid, gp, after):
    return pl.pallas_call(
        partial_kernel,
        out_shape=[sds(16, WIDTH)] * 2 + [sds(2, 64, WIDTH), sds(2, 48, WIDTH)],
        in_specs=[SMEM] + [VMEM] * 4 + [ANY],
        out_specs=[VMEM] * 4,
        scratch_shapes=[pltpu.VMEM((DB, BLK, BLK), F32)],
        compiler_params=pltpu.CompilerParams(vmem_limit_bytes=24 * MB),
        cost_estimate=pl.CostEstimate(flops=1 << 31, bytes_accessed=12 * MB, transcendentals=0),
        name="partial",
    )(meta, w1, w2, hid, gp, after)


def run_weight(meta, hid, gp, tok, grad):
    return pl.pallas_call(
        weight_kernel,
        out_shape=[sds(4, CAP - FEW, 16, BLK)] * 2 + [sds(2, CAP + FEW, 16, BLK)] * 4,
        in_specs=[SMEM] + [VMEM] * 4,
        out_specs=[VMEM] * 2 + [ANY] * 4,
        scratch_shapes=[
            pltpu.VMEM((4, 2, CAP + FEW, 16, BLK), BF16),
            pltpu.SemaphoreType.DMA((4,)),
        ],
        compiler_params=pltpu.CompilerParams(vmem_limit_bytes=16 * MB),
        cost_estimate=pl.CostEstimate(flops=1 << 31, bytes_accessed=8 * MB, transcendentals=0),
        name="weight",
    )(meta, hid, gp, tok, grad)


def run_chunk(core, *rows):
    return pl.pallas_call(
        chunk_kernel,
        out_shape=[sds(16, WIDTH)] * 2,
        in_specs=[SMEM] + [VMEM] * 4,
        out_specs=[VMEM] * 2,
        compiler_params=pltpu.CompilerParams(vmem_limit_bytes=8 * MB),
        name="chunk",
    )(core, *rows)


def add(terms, after=(), out=BF16, token=False):
    terms = [t if isinstance(t, tuple) else (t, ()) for t in terms]
    count = len(terms)

    def kernel(*refs):
        total = None
        for ref, (_, index) in zip(refs, terms):
            v = (ref[index] if index else ref[...]).astype(F32)
            total = v if total is None else total + v
        refs[count + len(after)][...] = total.astype(out)
        if token:
            refs[-1][...] = jnp.zeros((8, BLK), F32)

    shape = jax.eval_shape(lambda a: a[terms[0][1]], terms[0][0]).shape
    outs = [jax.ShapeDtypeStruct(shape, out)]
    if token:
        outs.append(jax.ShapeDtypeStruct((8, BLK), F32))
    done = pl.pallas_call(
        kernel,
        out_shape=outs,
        in_specs=[VMEM] * count + [ANY] * len(after),
        out_specs=[VMEM] * len(outs),
        compiler_params=pltpu.CompilerParams(vmem_limit_bytes=12 * MB),
        cost_estimate=pl.CostEstimate(flops=1, bytes_accessed=MB, transcendentals=0),
        name="add",
    )(*(t[0] for t in terms), *after)
    return done if token else done[0]


def home_kernel(core, home, p, q, after, away, keep):
    low = core[0] == 0
    p = home[0, 48:].astype(F32) + p[...].astype(F32)
    q = home[1, 48:].astype(F32) + q[...].astype(F32)
    for which, t in enumerate((jnp.where(low, p, q), jnp.where(low, q, p))):
        first = jnp.concatenate([t[0:4], t[8:12]], axis=0)
        second = jnp.concatenate([t[4:8], t[12:16]], axis=0)
        keep[which] = jnp.where(low, first, second)
        away[which] = jnp.where(low, second, first).astype(BF16)


def half_kernel(mine, got, away, keep):
    for which in range(2):
        t = mine[which] + got[which].astype(F32)
        keep[which] = t[:4]
        away[which] = t[4:].astype(BF16)


def last_kernel(own, more, keep, got, first, second, whole):
    whole[...] = own[...] + more[...].astype(F32)
    for which, dst in enumerate((first, second)):
        dst[...] = (keep[which] + got[which].astype(F32)).astype(BF16)


def run_last(own, more, keep, got):
    return pl.pallas_call(
        last_kernel,
        out_shape=[sds(4, WIDTH)] * 2 + [jax.ShapeDtypeStruct((CAP, 16, BLK), F32)],
        in_specs=[VMEM] * 4,
        out_specs=[VMEM] * 3,
        compiler_params=pltpu.CompilerParams(vmem_limit_bytes=12 * MB),
        name="last",
    )(own, more, keep, got)


def run_home(home, p, q, after):
    core = lax.axis_index("c").astype(jnp.int32).reshape(1)
    return pl.pallas_call(
        home_kernel,
        out_shape=[sds(2, 8, WIDTH), jax.ShapeDtypeStruct((2, 8, WIDTH), F32)],
        in_specs=[SMEM] + [VMEM] * 3 + [ANY],
        out_specs=[VMEM] * 2,
        compiler_params=pltpu.CompilerParams(vmem_limit_bytes=12 * MB),
        name="home",
    )(core, home, p, q, after)


def run_half(mine, got):
    return pl.pallas_call(
        half_kernel,
        out_shape=[sds(2, 4, WIDTH), jax.ShapeDtypeStruct((2, 4, WIDTH), F32)],
        in_specs=[VMEM] * 2,
        out_specs=[VMEM] * 2,
        compiler_params=pltpu.CompilerParams(vmem_limit_bytes=12 * MB),
        name="half",
    )(mine, got)


def swap(v, axis):
    return lax.ppermute(v, axis, [(0, 1), (1, 0)])


def ring(v, axis, n, sign):
    pairs = []
    for i in range(n):
        for c in range(2):
            step = sign if c == 0 else -sign
            pairs.append((i * 2 + c, ((i + step) % n) * 2 + c))
    if axis == "z":
        full = []
        for i in range(n):
            for y in range(2):
                for c in range(2):
                    step = sign if c == 0 else -sign
                    full.append(((i * 2 + y) * 2 + c, (((i + step) % n) * 2 + y) * 2 + c))
        return lax.ppermute(v, ("z", "yl", "c"), full)
    return lax.ppermute(v, (axis, "c"), pairs)


def f32(v):
    return v.astype(F32)


def narrow(v):
    return v.astype(BF16)


def tie(*values):
    return lax.optimization_barrier(values)


def gather_rows(tokens, grads, early):
    x = jnp.stack([tokens, grads])
    y = swap(x, "yl")
    core = lax.axis_index("c").astype(jnp.int32).reshape(1)
    p0, q0 = run_chunk(core, x, swap(x, "c"), y, swap(y, "c"))
    w1, w2, count1, count2 = early[0], early[1], early[4], early[7]
    meta = prepare(*tie(p0, *early[2:])[1:])
    p = [p0, ring(p0, "z", 8, 1)]
    q = [q0, ring(q0, "z", 8, 1)]
    p[1], meta = tie(p[1], meta)
    p[1], w1, w2 = tie(p[1], w1, w2)
    slot = jnp.arange(CAP, dtype=jnp.int32)[:, None, None]
    live1 = jnp.where(slot < count1[0], w1, jnp.zeros_like(w1))
    live2 = jnp.where(slot < count2[0], w2, jnp.zeros_like(w2))
    p.append(ring(p[1], "z", 8, 1))
    q.append(ring(q[1], "z", 8, 1))
    p[2], live1, live2 = tie(p[2], live1, live2)
    p.append(ring(p[2], "z", 8, 1))
    q.append(ring(q[2], "z", 8, 1))
    p.append(ring(p[-1], "z", 8, 1))
    return p + q + [swap(v, "c") for v in p[1:]] + [swap(v, "c") for v in q[1:]], (live1, live2, meta)


def reduce_all(far, got_far, near, got, mine1, across1, parts):
    def part(stream, k):
        here = (stream, slice(16 * (3 - k), 16 * (4 - k)))
        return [(near, here), (got, here)]

    op = add([far, got_far])
    p = ring(op, "z", 8, 1)
    op = add(part(1, 3), [op])
    q = ring(op, "z", 8, 1)
    xa = ring(parts[2], "x", 4, 1)
    xb = ring(parts[3], "x", 4, -1)

    op = add([parts[1], xa], [op])
    xa = ring(op, "x", 4, 1)

    op = add(part(0, 3) + [p], [op])
    p = ring(op, "z", 8, 1)
    op = add(part(1, 2) + [q], [op])
    q = ring(op, "z", 8, 1)

    op = add(part(0, 2) + [p], [op])
    p = ring(op, "z", 8, 1)
    op = add(part(1, 1) + [q], [op])
    q = ring(op, "z", 8, 1)

    op = add([(parts[0], (1,)), (xa, (1,)), (xb, (1,))], [op])
    across2 = swap(op, "yh")

    op = add(part(0, 1) + [p], [op])
    p = ring(op, "z", 8, 1)

    op = add([(mine1, (2,)), (across1, (2,))], [op])
    xc = ring(op, "x", 4, 1)
    op = add([(mine1, (3,)), (across1, (3,))], [op])
    xd = ring(op, "x", 4, -1)

    terms = [(parts[0], (0,)), (xa, (0,)), (xb, (0,)), across2]
    grad_w2, ready = add(terms, [op], F32, True)
    away, keep = run_home(near, p, q, ready)
    got = swap(away, "c")
    op = add([(mine1, (1,)), (across1, (1,)), xc], [away, xd])
    xc = ring(op, "x", 4, 1)
    away, keep = run_half(keep, got)
    got = swap(away, "yl")
    own = add([(mine1, (0,)), (across1, (0,)), xd], [away], F32)
    layer_out, grad_tokens, grad_w1 = run_last(own, xc, keep, got)
    return layer_out, grad_tokens, grad_w1, grad_w2


def prepare(w1_rows, w1_cols, w1_count, w2_rows, w2_cols, w2_count):
    stripe = (lax.axis_index("z") * 2 + lax.axis_index("yl")) * 2 + lax.axis_index("c")
    here = jnp.stack([lax.axis_index("c"), lax.axis_index("x"), lax.axis_index("yh")])
    meta = jnp.concatenate(
        [
            w1_rows,
            jnp.clip(w1_cols - stripe * SB, 0, SB - 1),
            jnp.clip(w2_rows - stripe * SB, 0, SB - 1),
            w2_cols,
            w1_count,
            w2_count,
            here.astype(jnp.int32),
        ]
    )
    return meta


def shards(tokens, grads, w1, w1_rows, w1_cols, w1_count, w2, w2_rows, w2_cols, w2_count):
    early = (w1, w2, w1_rows, w1_cols, w1_count, w2_rows, w2_cols, w2_count)
    pieces, (live1, live2, meta) = gather_rows(tokens, grads, early)
    hid, gp, tok, grad = run_hidden(meta, live1, live2, pieces)
    mine1, away1, *parts = run_weight(meta, hid, gp, tok, grad)
    far, send_far, near, send = run_partial(meta, live1, live2, hid, gp, mine1)
    got_far = swap(send_far, "c")
    got = swap(send, "c")
    layer_out, grad_tokens, grad_w1, grad_w2 = reduce_all(
        far, got_far, near, got, mine1, swap(away1, "yh"), parts
    )
    return layer_out, grad_tokens, grad_w1, grad_w2


def solution(mesh):
    fine = Mesh(mesh.devices.reshape(SIZES), AXES)
    rows = P(AXES, None)
    stripe = ("z", "yl", "c")
    flat = P(stripe)
    blocks = P(stripe, None, None)
    in_specs = (rows, rows, blocks, flat, flat, flat, blocks, flat, flat, flat)
    grads = P(stripe, ("yh", "x"), None)
    out_specs = (rows, rows, grads, grads)
    return jax.shard_map(
        shards, mesh=fine, in_specs=in_specs, out_specs=out_specs, check_vma=False
    )
```

```python
import jax
import jax.numpy as jnp
from jax import lax
from jax.experimental import pallas as pl
from jax.experimental.pallas import tpu as pltpu
from jax.sharding import Mesh
from jax.sharding import PartitionSpec as P

AXES = ("yh", "x", "z", "yl", "c")
SIZES = (2, 4, 8, 2, 2)
BLK = 128
SB = 4
CAP = 64
DB = 64
WIDTH = DB * BLK
F32 = jnp.float32
BF16 = jnp.bfloat16
FEW = 0
R1, C1, R2, C2, LIVE1, LIVE2, CORE, PX, PYH = 0, 64, 128, 192, 256, 257, 258, 259, 260
MB = 1024 * 1024


def gelu_pair(v):
    a = 0.7978845608028654
    b = 0.044715
    v2 = v * v
    t = jnp.tanh(a * v * (1.0 + b * v2))
    half = 0.5 * (1.0 + t)
    slope = half + 0.5 * v * (1.0 - t * t) * (a * (1.0 + 3.0 * b * v2))
    return v * half, slope


def lanes(block):
    return pl.ds(pl.multiple_of(block * BLK, BLK), BLK)


def loop(body, start=0, group=64):
    def step(i, carry):
        for j in range(group):
            body(start + i * group + j)
        return carry

    lax.fori_loop(0, (CAP - start) // group, step, 0)


def dot(a, b, dims):
    return lax.dot_general(a, b, (dims, ((), ())), preferred_element_type=F32)


def hidden_kernel(meta, w1, w2, *refs):
    p, q, pm, qm = refs[:5], refs[5:9], refs[9:13], refs[13:16]
    hid, gp, tok, grad, pre, back = refs[16:]
    low = meta[CORE] == 0

    def put(unit, a, b):
        rows = slice(16 * unit, 16 * unit + 16)
        a, b = a[...], b[...]
        tok[rows] = jnp.where(low, a, b)
        grad[rows] = jnp.where(low, b, a)

    put(0, p[4], pm[3])
    for i, k in enumerate((3, 2, 1)):
        put(1 + i, p[k], q[k])
        put(4 + i, qm[k - 1], pm[k - 1])
    put(7, p[0], q[0])
    pre[...] = jnp.zeros_like(pre)
    back[...] = jnp.zeros_like(back)

    def up(s):
        pre[meta[C1 + s]] += dot(tok[:, lanes(meta[R1 + s])], w1[s], ((1,), (0,)))

    loop(up)

    def down(s):
        back[meta[R2 + s]] += dot(grad[:, lanes(meta[C2 + s])], w2[s], ((1,), (1,)))

    loop(down)
    for k in range(SB):
        h, slope = gelu_pair(pre[k])
        hid[k] = h.astype(BF16)
        gp[k] = (back[k] * slope).astype(BF16)


def partial_kernel(meta, w1, w2, hid, gp, after, far, send_far, near, send, acc):
    core = meta[CORE]

    def finish(stream):
        for b in range(DB):
            here = slice(b * BLK, (b + 1) * BLK)
            v = acc[b].astype(BF16)
            if stream == 0:
                far[:, here] = v[:16]
            else:
                send_far[:, here] = v[:16]
            send[1 - stream, :, here] = v[16:64]
            near[stream, :, here] = v[64:]

    def finish_array(which):
        pl.when(core == which)(lambda: finish(0))
        pl.when(core != which)(lambda: finish(1))

    acc[...] = jnp.zeros_like(acc)

    def out(s):
        acc[meta[C2 + s]] += dot(hid[meta[R2 + s]], w2[s], ((1,), (0,)))

    loop(out)
    finish_array(0)
    acc[...] = jnp.zeros_like(acc)

    def tback(s):
        acc[meta[R1 + s]] += dot(gp[meta[C1 + s]], w1[s], ((1,), (1,)))

    loop(tback)
    finish_array(1)


def rel_x(meta, j):
    d = j % 4 - meta[PX]
    return jnp.where(meta[CORE] == 0, d, -d) & 3


def weight_kernel(meta, hid, gp, tok, grad, near, far, *refs):
    outs, stage, sem = refs[:4], refs[4], refs[5]
    n1 = meta[LIVE1]
    n2 = meta[LIVE2]
    pyh = meta[PYH]

    def put(slot, v):
        for j in range(8):
            stage[rel_x(meta, j), (j // 4) ^ pyh, slot] = v[16 * j : 16 * j + 16]

    def second(s):
        v = dot(hid[meta[R2 + s]], grad[:, lanes(meta[C2 + s])], ((0,), (0,)))
        put(s, jnp.where(s < n2, v, 0.0).astype(BF16))

    def first(s):
        v = dot(tok[:, lanes(meta[R1 + s])], gp[meta[C1 + s]], ((0,), (0,)))
        return jnp.where(s < n1, v, 0.0).astype(BF16)

    loop(second)
    for s in range(FEW):
        put(CAP + s, first(s))
    copies = [pltpu.make_async_copy(stage.at[k], outs[k], sem.at[k]) for k in range(4)]
    for cp in copies:
        cp.start()

    def rest(s):
        v = first(s)
        for j in range(4):
            k = rel_x(meta, j)
            low, high = v[16 * j : 16 * j + 16], v[16 * j + 64 : 16 * j + 80]
            near[k, s - FEW] = jnp.where(pyh == 0, low, high)
            far[k, s - FEW] = jnp.where(pyh == 0, high, low)

    loop(rest, FEW)
    for cp in copies:
        cp.wait()


def chunk_kernel(core, x, xc, y, yc, p, q):
    low = core[0] == 0
    both = []
    for which in range(2):
        rows = []
        for a, b in ((x, xc), (y, yc)):
            here = slice(4 * which, 4 * which + 4)
            a, b = a[...].astype(F32)[here], b[...].astype(F32)[here]
            rows += [jnp.where(low, a, b), jnp.where(low, b, a)]
        both.append(jnp.concatenate(rows, axis=0))
    p[...] = jnp.where(low, both[0], both[1]).astype(BF16)
    q[...] = jnp.where(low, both[1], both[0]).astype(BF16)


VMEM = pl.BlockSpec(memory_space=pltpu.VMEM)
SMEM = pl.BlockSpec(memory_space=pltpu.SMEM)
ANY = pl.BlockSpec(memory_space=pl.ANY)


def sds(*shape):
    return jax.ShapeDtypeStruct(shape, BF16)


def run_hidden(meta, w1, w2, pieces):
    return pl.pallas_call(
        hidden_kernel,
        out_shape=[sds(SB, BLK, BLK)] * 2 + [sds(BLK, WIDTH)] * 2,
        in_specs=[SMEM, VMEM, VMEM] + [VMEM] * 16,
        out_specs=[VMEM] * 4,
        scratch_shapes=[pltpu.VMEM((SB, BLK, BLK), F32)] * 2,
        compiler_params=pltpu.CompilerParams(vmem_limit_bytes=24 * MB),
        cost_estimate=pl.CostEstimate(flops=1 << 31, bytes_accessed=12 * MB, transcendentals=1 << 16),
        name="hidden",
    )(meta, w1, w2, *pieces)


def run_partial(meta, w1, w2, hid, gp, after):
    return pl.pallas_call(
        partial_kernel,
        out_shape=[sds(16, WIDTH)] * 2 + [sds(2, 64, WIDTH), sds(2, 48, WIDTH)],
        in_specs=[SMEM] + [VMEM] * 4 + [ANY],
        out_specs=[VMEM] * 4,
        scratch_shapes=[pltpu.VMEM((DB, BLK, BLK), F32)],
        compiler_params=pltpu.CompilerParams(vmem_limit_bytes=24 * MB),
        cost_estimate=pl.CostEstimate(flops=1 << 31, bytes_accessed=12 * MB, transcendentals=0),
        name="partial",
    )(meta, w1, w2, hid, gp, after)


def run_weight(meta, hid, gp, tok, grad):
    return pl.pallas_call(
        weight_kernel,
        out_shape=[sds(4, CAP - FEW, 16, BLK)] * 2 + [sds(2, CAP + FEW, 16, BLK)] * 4,
        in_specs=[SMEM] + [VMEM] * 4,
        out_specs=[VMEM] * 2 + [ANY] * 4,
        scratch_shapes=[
            pltpu.VMEM((4, 2, CAP + FEW, 16, BLK), BF16),
            pltpu.SemaphoreType.DMA((4,)),
        ],
        compiler_params=pltpu.CompilerParams(vmem_limit_bytes=16 * MB),
        cost_estimate=pl.CostEstimate(flops=1 << 31, bytes_accessed=8 * MB, transcendentals=0),
        name="weight",
    )(meta, hid, gp, tok, grad)


def run_chunk(core, *rows):
    return pl.pallas_call(
        chunk_kernel,
        out_shape=[sds(16, WIDTH)] * 2,
        in_specs=[SMEM] + [VMEM] * 4,
        out_specs=[VMEM] * 2,
        compiler_params=pltpu.CompilerParams(vmem_limit_bytes=8 * MB),
        name="chunk",
    )(core, *rows)


def add(terms, after=(), out=BF16, token=False):
    terms = [t if isinstance(t, tuple) else (t, ()) for t in terms]
    count = len(terms)

    def kernel(*refs):
        total = None
        for ref, (_, index) in zip(refs, terms):
            v = (ref[index] if index else ref[...]).astype(F32)
            total = v if total is None else total + v
        refs[count + len(after)][...] = total.astype(out)
        if token:
            refs[-1][...] = jnp.zeros((8, BLK), F32)

    shape = jax.eval_shape(lambda a: a[terms[0][1]], terms[0][0]).shape
    outs = [jax.ShapeDtypeStruct(shape, out)]
    if token:
        outs.append(jax.ShapeDtypeStruct((8, BLK), F32))
    done = pl.pallas_call(
        kernel,
        out_shape=outs,
        in_specs=[VMEM] * count + [ANY] * len(after),
        out_specs=[VMEM] * len(outs),
        compiler_params=pltpu.CompilerParams(vmem_limit_bytes=12 * MB),
        cost_estimate=pl.CostEstimate(flops=1, bytes_accessed=MB, transcendentals=0),
        name="add",
    )(*(t[0] for t in terms), *after)
    return done if token else done[0]


def home_kernel(core, home, p, q, after, away, keep):
    low = core[0] == 0
    p = home[0, 48:].astype(F32) + p[...].astype(F32)
    q = home[1, 48:].astype(F32) + q[...].astype(F32)
    for which, t in enumerate((jnp.where(low, p, q), jnp.where(low, q, p))):
        first = jnp.concatenate([t[0:4], t[8:12]], axis=0)
        second = jnp.concatenate([t[4:8], t[12:16]], axis=0)
        keep[which] = jnp.where(low, first, second)
        away[which] = jnp.where(low, second, first).astype(BF16)


def half_kernel(mine, got, away, keep):
    for which in range(2):
        t = mine[which] + got[which].astype(F32)
        keep[which] = t[:4]
        away[which] = t[4:].astype(BF16)


def last_kernel(own, more, keep, got, first, second, whole):
    whole[...] = own[...] + more[...].astype(F32)
    for which, dst in enumerate((first, second)):
        dst[...] = (keep[which] + got[which].astype(F32)).astype(BF16)


def run_last(own, more, keep, got):
    return pl.pallas_call(
        last_kernel,
        out_shape=[sds(4, WIDTH)] * 2 + [jax.ShapeDtypeStruct((CAP, 16, BLK), F32)],
        in_specs=[VMEM] * 4,
        out_specs=[VMEM] * 3,
        compiler_params=pltpu.CompilerParams(vmem_limit_bytes=12 * MB),
        name="last",
    )(own, more, keep, got)


def run_home(home, p, q, after):
    core = lax.axis_index("c").astype(jnp.int32).reshape(1)
    return pl.pallas_call(
        home_kernel,
        out_shape=[sds(2, 8, WIDTH), jax.ShapeDtypeStruct((2, 8, WIDTH), F32)],
        in_specs=[SMEM] + [VMEM] * 3 + [ANY],
        out_specs=[VMEM] * 2,
        compiler_params=pltpu.CompilerParams(vmem_limit_bytes=12 * MB),
        name="home",
    )(core, home, p, q, after)


def run_half(mine, got):
    return pl.pallas_call(
        half_kernel,
        out_shape=[sds(2, 4, WIDTH), jax.ShapeDtypeStruct((2, 4, WIDTH), F32)],
        in_specs=[VMEM] * 2,
        out_specs=[VMEM] * 2,
        compiler_params=pltpu.CompilerParams(vmem_limit_bytes=12 * MB),
        name="half",
    )(mine, got)


def swap(v, axis):
    return lax.ppermute(v, axis, [(0, 1), (1, 0)])


def ring(v, axis, n, sign):
    pairs = []
    for i in range(n):
        for c in range(2):
            step = sign if c == 0 else -sign
            pairs.append((i * 2 + c, ((i + step) % n) * 2 + c))
    if axis == "z":
        full = []
        for i in range(n):
            for y in range(2):
                for c in range(2):
                    step = sign if c == 0 else -sign
                    full.append(((i * 2 + y) * 2 + c, (((i + step) % n) * 2 + y) * 2 + c))
        return lax.ppermute(v, ("z", "yl", "c"), full)
    return lax.ppermute(v, (axis, "c"), pairs)


def f32(v):
    return v.astype(F32)


def narrow(v):
    return v.astype(BF16)


def tie(*values):
    return lax.optimization_barrier(values)


def gather_rows(tokens, grads, early):
    x = jnp.concatenate([tokens, grads], axis=0)
    y = swap(x, "yl")
    core = lax.axis_index("c").astype(jnp.int32).reshape(1)
    p0, q0 = run_chunk(core, x, swap(x, "c"), y, swap(y, "c"))
    w1, w2, count1, count2 = early[0], early[1], early[4], early[7]
    meta = prepare(*tie(p0, *early[2:])[1:])
    p = [p0, ring(p0, "z", 8, 1)]
    q = [q0, ring(q0, "z", 8, 1)]
    p[1], meta = tie(p[1], meta)
    p[1], w1, w2 = tie(p[1], w1, w2)
    slot = jnp.arange(CAP, dtype=jnp.int32)[:, None, None]
    live1 = jnp.where(slot < count1[0], w1, jnp.zeros_like(w1))
    live2 = jnp.where(slot < count2[0], w2, jnp.zeros_like(w2))
    p.append(ring(p[1], "z", 8, 1))
    q.append(ring(q[1], "z", 8, 1))
    p[2], live1, live2 = tie(p[2], live1, live2)
    p.append(ring(p[2], "z", 8, 1))
    q.append(ring(q[2], "z", 8, 1))
    p.append(ring(p[-1], "z", 8, 1))
    return p + q + [swap(v, "c") for v in p[1:]] + [swap(v, "c") for v in q[1:]], (live1, live2, meta)


def reduce_all(far, got_far, near, got, mine1, across1, parts):
    def part(stream, k):
        here = (stream, slice(16 * (3 - k), 16 * (4 - k)))
        return [(near, here), (got, here)]

    op = add([far, got_far])
    p = ring(op, "z", 8, 1)
    op = add(part(1, 3), [op])
    q = ring(op, "z", 8, 1)
    xa = ring(parts[2], "x", 4, 1)
    xb = ring(parts[3], "x", 4, -1)

    op = add([parts[1], xa], [op])
    xa = ring(op, "x", 4, 1)

    op = add(part(0, 3) + [p], [op])
    p = ring(op, "z", 8, 1)
    op = add(part(1, 2) + [q], [op])
    q = ring(op, "z", 8, 1)

    op = add(part(0, 2) + [p], [op])
    p = ring(op, "z", 8, 1)
    op = add(part(1, 1) + [q], [op])
    q = ring(op, "z", 8, 1)

    op = add([(parts[0], (1,)), (xa, (1,)), (xb, (1,))], [op])
    across2 = swap(op, "yh")

    op = add(part(0, 1) + [p], [op])
    p = ring(op, "z", 8, 1)

    op = add([(mine1, (2,)), (across1, (2,))], [op])
    xc = ring(op, "x", 4, 1)
    op = add([(mine1, (3,)), (across1, (3,))], [op])
    xd = ring(op, "x", 4, -1)

    terms = [(parts[0], (0,)), (xa, (0,)), (xb, (0,)), across2]
    grad_w2, ready = add(terms, [op], F32, True)
    away, keep = run_home(near, p, q, ready)
    got = swap(away, "c")
    op = add([(mine1, (1,)), (across1, (1,)), xc], [away, xd])
    xc = ring(op, "x", 4, 1)
    away, keep = run_half(keep, got)
    got = swap(away, "yl")
    own = add([(mine1, (0,)), (across1, (0,)), xd], [away], F32)
    layer_out, grad_tokens, grad_w1 = run_last(own, xc, keep, got)
    return layer_out, grad_tokens, grad_w1, grad_w2


def prepare(w1_rows, w1_cols, w1_count, w2_rows, w2_cols, w2_count):
    stripe = (lax.axis_index("z") * 2 + lax.axis_index("yl")) * 2 + lax.axis_index("c")
    here = jnp.stack([lax.axis_index("c"), lax.axis_index("x"), lax.axis_index("yh")])
    meta = jnp.concatenate(
        [
            w1_rows,
            jnp.clip(w1_cols - stripe * SB, 0, SB - 1),
            jnp.clip(w2_rows - stripe * SB, 0, SB - 1),
            w2_cols,
            w1_count,
            w2_count,
            here.astype(jnp.int32),
        ]
    )
    return meta


def shards(tokens, grads, w1, w1_rows, w1_cols, w1_count, w2, w2_rows, w2_cols, w2_count):
    early = (w1, w2, w1_rows, w1_cols, w1_count, w2_rows, w2_cols, w2_count)
    pieces, (live1, live2, meta) = gather_rows(tokens, grads, early)
    hid, gp, tok, grad = run_hidden(meta, live1, live2, pieces)
    mine1, away1, *parts = run_weight(meta, hid, gp, tok, grad)
    far, send_far, near, send = run_partial(meta, live1, live2, hid, gp, mine1)
    got_far = swap(send_far, "c")
    got = swap(send, "c")
    layer_out, grad_tokens, grad_w1, grad_w2 = reduce_all(
        far, got_far, near, got, mine1, swap(away1, "yh"), parts
    )
    return layer_out, grad_tokens, grad_w1, grad_w2


def solution(mesh):
    fine = Mesh(mesh.devices.reshape(SIZES), AXES)
    rows = P(AXES, None)
    stripe = ("z", "yl", "c")
    flat = P(stripe)
    blocks = P(stripe, None, None)
    in_specs = (rows, rows, blocks, flat, flat, flat, blocks, flat, flat, flat)
    grads = P(stripe, ("yh", "x"), None)
    out_specs = (rows, rows, grads, grads)
    return jax.shard_map(
        shards, mesh=fine, in_specs=in_specs, out_specs=out_specs, check_vma=False
    )
```
